128 devices in a mesh: seq: 32 (over z, y, core), enc: 4 (over x).
Axes of the slice: x: 4, y: 4, z: 4, core: 2. Of those that a mesh axis runs over, the one named last changes fastest.
Arguments:
- enc_tiles: bfloat16 [32, 4, 1601, 1280], P('seq', 'enc'), may hold values from -6 to 6
- kv_weight: bfloat16 [1280, 1024], replicated, may hold values from -0.15625 to 0.15625
- q_cross: bfloat16 [4096, 4096], P('seq', 'enc'), may hold values from -210 to 210
- q_self: bfloat16 [4096, 4096], P('seq', 'enc'), may hold values from -210 to 210
- self_cache: bfloat16 [4, 256, 4096], P('enc', 'seq'), may hold values from -6 to 6
- image_range: int32 [64, 2], P('seq'), may hold values from 0 to 32, as said below
- image_tiles: int32 [32], replicated, may hold values from 1 to 4
Outputs:
- cross_context: bfloat16 [4096, 4096], P('seq', 'enc')
- self_context: bfloat16 [4096, 4096], P('seq', 'enc')
- cache_seq: bfloat16 [4, 256, 4096], P('enc', None, 'seq')
The draws below stay inside these ranges and needn't reach their ends.
Inputs may be any that keep to these rules, and one draw needn't show every extreme that they name: With s = c // 2, span c sees one or two images: s - 1 <= image_range[c, 0] < image_range[c, 1] <= s + 1.
All inputs are finite; a program needn't handle non-finite values.
Results may differ from the reference program's by a relative error of at most 0.012.
The reference program's roundings to bfloat16 on the way count: a program that leaves them out, or rounds other values in their place, can miss the bound.
Values may be sent and summed in bfloat16 or wider, within the bound.
No kernel may reach another device: no remote copies, remote signals or barrier semaphores. Data moves between devices by JAX's collectives and lax.ppermute only.
A program may use at most 128 MiB of HBM per device.

```python
import math
import jax
import jax.numpy as jnp
from jax import lax

HD = 128
HQ = 32
KVH = 4
ENC_W = 1280
TILE_TOK = 1601
TILES = 4
SPAN = 64
TOK_DEV = 128
TOKENS = 4096
SPANS = 64
IMAGES = 32


def draw_q_cross(key, part):
    key = jax.random.fold_in(key, 11)
    values = jnp.clip(jax.random.normal(key, (TOKENS, HQ * HD), jnp.float32), -6.0, 6.0)
    return values.astype(jnp.bfloat16)


def draw_q_self(key, part):
    key = jax.random.fold_in(key, 12)
    values = jnp.clip(jax.random.normal(key, (TOKENS, HQ * HD), jnp.float32), -6.0, 6.0)
    return values.astype(jnp.bfloat16)


def draw_image_range(key, part):
    key = jax.random.fold_in(key, 13)
    span_index = jnp.arange(SPANS, dtype=jnp.int32)
    text_index = span_index // (TOK_DEV // SPAN)
    span_kind = jax.random.randint(key, (SPANS,), 0, 3)
    span_kind = jnp.where(text_index == 0, 2, span_kind)
    span_kind = jnp.where(span_index == SPANS - 1, 2, span_kind)
    lower_image = jnp.where(span_kind == 2, text_index, text_index - 1)
    upper_image = jnp.where(span_kind == 0, text_index, text_index + 1)
    return jnp.stack([lower_image, upper_image], 1).astype(jnp.int32)


def draw_image_tiles(key, part):
    key = jax.random.fold_in(key, 14)
    key_count, key_order = jax.random.split(key)
    tile_count = jax.random.randint(key_count, (IMAGES,), 1, TILES + 1)
    shuffled = jax.random.permutation(key_order, IMAGES)
    tile_count = tile_count.at[shuffled[0]].set(TILES).at[shuffled[1]].set(1)
    return tile_count.astype(jnp.int32)


def levels(stream_key, dims, shards, low, high):
    loudness = 1.0
    for axis_at, shards_of in shards:
        draws = jax.random.uniform(jax.random.fold_in(jax.random.fold_in(stream_key, 6), axis_at), (shards_of,), jnp.float32, low / len(shards), high / len(shards))
        loudness = loudness * jnp.repeat(jnp.exp(draws), dims[axis_at] // shards_of).reshape((-1,) + (1,) * (len(dims) - 1 - axis_at))
    return loudness


def centred(stream_key, shape, scale, most, shards=(), kind=jnp.bfloat16):
    entries = scale * jax.random.normal(stream_key, shape, jnp.float32)
    if shards:
        entries = entries * levels(stream_key, shape, shards, -0.22, 0.18)
    return jnp.clip(entries, -most, most).astype(kind)


def setup_inputs(seed: int = 0) -> dict:
    keys = jax.random.split(jax.random.key(seed), 8)
    enc_tiles = centred(keys[0], (IMAGES, TILES, TILE_TOK, ENC_W), 1.0, 6.0, ((0, 32), (1, 4)))
    kv_weight = centred(keys[1], (ENC_W, KVH * 2 * HD), ENC_W ** -0.5, 0.15625)
    q_cross = draw_q_cross(jax.random.fold_in(keys[7], 71), 0)
    q_self = draw_q_self(jax.random.fold_in(keys[7], 71), 0)
    self_cache = centred(keys[4], (KVH, 2 * HD, TOKENS), 1.0, 6.0, ((0, 4), (1, 32)))
    image_range = draw_image_range(jax.random.fold_in(keys[7], 71), 0)
    image_tiles = draw_image_tiles(jax.random.fold_in(keys[7], 71), 0)
    return dict(enc_tiles=enc_tiles, kv_weight=kv_weight, q_cross=q_cross, q_self=q_self, self_cache=self_cache, image_range=image_range, image_tiles=image_tiles)


NEG_FILL = -1e+30

def masked_attend(query_rows, key_rows, value_rows, allowed):
    scores = jnp.einsum('grd,kd->grk', query_rows, key_rows) * (1.0 / math.sqrt(HD))
    guarded = jnp.where(allowed[None], scores, NEG_FILL)
    row_max = lax.optimization_barrier(jnp.max(guarded, axis=-1, keepdims=True))
    exponent = jnp.where(allowed[None], jnp.exp(guarded - row_max), 0.0)
    row_sum = lax.optimization_barrier(jnp.sum(exponent, axis=-1))
    rounded = lax.optimization_barrier(exponent.astype(jnp.bfloat16))
    weights = rounded.astype(query_rows.dtype)
    mixed = jnp.einsum('grk,kd->grd', weights, value_rows)
    return mixed / row_sum[..., None]

def reference(enc_tiles, kv_weight, q_cross, q_self, self_cache, image_range, image_tiles):
    weight_full = kv_weight.astype(jnp.float32)
    group_size = HQ // KVH

    def project_image(one_image):
        flat_rows = one_image.reshape(TILES * TILE_TOK, ENC_W).astype(jnp.float32)
        return jnp.einsum('se,ec->sc', flat_rows, weight_full).astype(jnp.bfloat16)
    image_kv = lax.map(project_image, enc_tiles)
    key_width = TILES * TILE_TOK
    positions = jnp.arange(key_width, dtype=jnp.int32)

    def cross_span(span_index):
        lower_image = image_range[span_index, 0]
        upper_image = image_range[span_index, 1]
        first_image = jnp.clip(lower_image, 0, IMAGES - 2).astype(jnp.int32)
        image_pair = lax.dynamic_slice_in_dim(image_kv, first_image, 2, 0).astype(jnp.float32)
        image_pair = image_pair.reshape(2 * key_width, KVH, 2, HD)
        image_ids = first_image + jnp.arange(2, dtype=jnp.int32)
        live_tokens = image_tiles[image_ids] * TILE_TOK
        live_image = (image_ids >= lower_image) & (image_ids < upper_image)
        column_ok = (live_image[:, None] & (positions[None, :] < live_tokens[:, None])).reshape(2 * key_width)
        allowed = jnp.broadcast_to(column_ok[None, :], (SPAN, 2 * key_width))
        row_start = (span_index * SPAN).astype(jnp.int32)
        query_block = lax.dynamic_slice_in_dim(q_cross, row_start, SPAN, 0).astype(jnp.float32)
        query_block = query_block.reshape(SPAN, KVH, group_size, HD)
        head_outputs = []
        for head_index in range(KVH):
            mixed = masked_attend(jnp.transpose(query_block[:, head_index], (1, 0, 2)), image_pair[:, head_index, 0], image_pair[:, head_index, 1], allowed)
            head_outputs.append(jnp.transpose(mixed, (1, 0, 2)))
        return jnp.stack(head_outputs, 1).reshape(SPAN, HQ * HD)
    cross_context = lax.map(cross_span, jnp.arange(SPANS, dtype=jnp.int32)).reshape(TOKENS, HQ * HD).astype(jnp.bfloat16)
    query_size = min(512, TOKENS)
    key_pos = jnp.arange(TOKENS, dtype=jnp.int32)
    cache_full = self_cache.astype(jnp.float32)

    def self_block(block_index):
        row_start = (block_index * query_size).astype(jnp.int32)
        query_block = lax.dynamic_slice_in_dim(q_self, row_start, query_size, 0).astype(jnp.float32)
        query_block = query_block.reshape(query_size, KVH, group_size, HD)
        row_pos = row_start + jnp.arange(query_size, dtype=jnp.int32)
        allowed = key_pos[None, :] <= row_pos[:, None]
        head_outputs = []
        for head_index in range(KVH):
            mixed = masked_attend(jnp.transpose(query_block[:, head_index], (1, 0, 2)), cache_full[head_index, :HD].T, cache_full[head_index, HD:].T, allowed)
            head_outputs.append(jnp.transpose(mixed, (1, 0, 2)))
        return jnp.stack(head_outputs, 1).reshape(query_size, HQ * HD)
    self_context = lax.map(self_block, jnp.arange(TOKENS // query_size, dtype=jnp.int32)).reshape(TOKENS, HQ * HD).astype(jnp.bfloat16)
    return (cross_context, self_context, self_cache)
```

```python
import functools
import math

import jax
import jax.numpy as jnp
from jax import lax
from jax.experimental import pallas as pl
from jax.experimental.pallas import tpu as pltpu
from jax.sharding import PartitionSpec as P

HD = 128
GROUP = 8
TOK = 128
WIDTH = GROUP * HD
STAT = 128
PACK = WIDTH + STAT
NEG = -1e30
EXP2_SCALE = math.log2(math.e) / math.sqrt(HD)
VMEM = 50 * 1024 * 1024
BF16 = jnp.bfloat16
F32 = jnp.float32


def params():
    return pltpu.CompilerParams(vmem_limit_bytes=VMEM)


def project_kernel(tiles_ref, x_ref, w_ref, o_ref, *, rows, step):
    live = lax.axis_index("enc") < tiles_ref[lax.axis_index("seq")]
    i = pl.program_id(0)

    @pl.when(live)
    def _():
        y = jnp.dot(x_ref[...], w_ref[...], preferred_element_type=F32).astype(BF16)
        row = lax.broadcasted_iota(jnp.int32, y.shape, 0) + i * step
        y = jnp.where(row < rows, y, jnp.zeros_like(y))
        for g in range(4):
            o_ref[g] = y[:, g * 2 * HD : (g + 1) * 2 * HD]


def project(tiles, x, w, padded, step):
    rows, depth = x.shape
    return pl.pallas_call(
        functools.partial(project_kernel, rows=rows, step=step),
        grid_spec=pltpu.PrefetchScalarGridSpec(
            num_scalar_prefetch=1,
            grid=(padded // step,),
            in_specs=[
                pl.BlockSpec((step, depth), lambda i, t: (i, 0)),
                pl.BlockSpec(w.shape, lambda i, t: (0, 0)),
            ],
            out_specs=pl.BlockSpec((4, step, 2 * HD), lambda i, t: (0, i, 0)),
        ),
        out_shape=jax.ShapeDtypeStruct((4, padded, 2 * HD), BF16),
        compiler_params=params(),
        cost_estimate=pl.CostEstimate(
            flops=2 * rows * depth * w.shape[1], bytes_accessed=10_000_000, transcendentals=0
        ),
        name="project",
    )(tiles, x, w)


def split_stat(lse):
    hi = lse.astype(BF16)
    rest = lse - hi.astype(F32)
    mid = rest.astype(BF16)
    low = (rest - mid.astype(F32)).astype(BF16)
    return hi, mid, low


def cross_kernel(tiles_ref, *refs, offsets, picks, rows, last_seq):
    count = len(offsets)
    q_refs = refs[:count]
    kv_hbm, o_ref, queries, kv, sems = refs[count:]
    enc = lax.axis_index("enc")
    seq = lax.axis_index("seq")
    live = enc < tiles_ref[seq]
    if last_seq is not None:
        live = live & (seq < last_seq)
    padded = kv.shape[1]

    @pl.when(jnp.logical_not(live))
    def _():
        o_ref[:, :, :WIDTH] = jnp.zeros((count, TOK, WIDTH), BF16)
        o_ref[:, :, WIDTH:] = jnp.full((count, TOK, STAT), NEG, BF16)

    @pl.when(live)
    def _():
        copies = []
        for b, offset in enumerate(offsets):
            copy = pltpu.make_async_copy(
                kv_hbm.at[lax.rem(enc + offset, 4)], kv.at[b], sems.at[b]
            )
            copy.start()
            copies.append(copy)
        for b in range(count):
            for h in range(GROUP):
                queries[b, h * TOK : (h + 1) * TOK] = q_refs[b][picks[b], :, h * HD : (h + 1) * HD]
        lanes = lax.broadcasted_iota(jnp.int32, (1, HD), 1)
        edge = jnp.where(lanes < rows - (padded - HD), 0.0, NEG)

        def one_block(b, carry):
            pltpu.make_async_copy(kv_hbm.at[0], kv.at[b], sems.at[b]).wait()
            keys = kv[b, :, :HD]
            values = jnp.concatenate([kv[b, :, HD:], jnp.ones((padded, HD), BF16)], 1)
            maxes = jnp.zeros((TOK, STAT), F32)
            sums = jnp.ones((TOK, STAT), F32)
            part = 4
            for c in range(GROUP // part):
                q = queries[b, c * part * TOK : (c + 1) * part * TOK]
                s = lax.dot_general(q, keys, (((1,), (1,)), ((), ())), preferred_element_type=F32)
                s = jnp.concatenate([s[:, : padded - HD], s[:, padded - HD :] + edge], 1)
                m = jnp.max(s, 1, keepdims=True)
                p = jnp.exp2((s - m) * EXP2_SCALE).astype(BF16)
                mixed = jnp.dot(p, values, preferred_element_type=F32)
                total = mixed[:, HD:]
                out = (mixed[:, :HD] * (1.0 / total)).astype(BF16)
                for a in range(part):
                    h = c * part + a
                    at = slice(a * TOK, (a + 1) * TOK)
                    o_ref[b, :, h * HD : (h + 1) * HD] = out[at]
                    here = lax.rem(lanes, GROUP) == h
                    maxes = jnp.where(here, m[at], maxes)
                    sums = jnp.where(here, total[at], sums)
            hi, mid, low = split_stat(maxes * EXP2_SCALE + jnp.log2(sums))
            stat = jnp.where(lanes < GROUP, hi, jnp.where(lanes < 2 * GROUP, mid, low))
            o_ref[b, :, WIDTH:] = stat
            return carry

        lax.fori_loop(0, count, one_block, 0)


def cross(tiles, sources, kv, offsets, rows, padded, last_seq=None):
    count = len(offsets)
    pairs = count * WIDTH * padded
    return pl.pallas_call(
        functools.partial(
            cross_kernel,
            offsets=offsets,
            picks=[0] * count,
            rows=rows,
            last_seq=last_seq,
        ),
        grid_spec=pltpu.PrefetchScalarGridSpec(
            num_scalar_prefetch=1,
            grid=(1,),
            in_specs=[
                pl.BlockSpec((1, TOK, WIDTH), functools.partial(lambda pick, i, t: (pick, 0, 0), pick))
                for _, pick in sources
            ]
            + [pl.BlockSpec(memory_space=pl.ANY)],
            out_specs=pl.BlockSpec((count, TOK, PACK), lambda i, t: (0, 0, 0)),
            scratch_shapes=[
                pltpu.VMEM((count, GROUP * TOK, HD), BF16),
                pltpu.VMEM((count, padded, 2 * HD), BF16),
                pltpu.SemaphoreType.DMA((count,)),
            ],
        ),
        out_shape=jax.ShapeDtypeStruct((count, TOK, PACK), BF16),
        compiler_params=params(),
        cost_estimate=pl.CostEstimate(
            flops=8 * pairs * HD, bytes_accessed=count * 1_400_000, transcendentals=pairs
        ),
        name="cross",
    )(tiles, *[a for a, _ in sources], kv)


def stat_of(packed):
    s = packed[:, WIDTH:].astype(F32)
    return s[:, :GROUP] + s[:, GROUP : 2 * GROUP] + s[:, 2 * GROUP : 3 * GROUP]


def merge_kernel(range_ref, own_ref, rest_ref, prev_ref, *o_refs):
    seq = lax.axis_index("seq")
    first = lax.broadcasted_iota(jnp.int32, (TOK, GROUP), 0) < TOK // 2
    sees = []
    for image in (seq, seq - 1):
        spans = [
            ((range_ref[c, 0] <= image) & (image < range_ref[c, 1])).astype(jnp.int32)
            for c in range(2)
        ]
        sees.append(jnp.where(first, spans[0], spans[1]) != 0)
    lanes = lax.broadcasted_iota(jnp.int32, (1, STAT), 1)
    for b in range(4):
        now = own_ref.at[0] if b == 0 else rest_ref.at[b - 1]
        before = prev_ref.at[b]
        l0 = jnp.where(sees[0], stat_of(now[...]), NEG)
        l1 = jnp.where(sees[1], stat_of(before[...]), NEG)
        top = jnp.maximum(l0, l1)
        w0 = jnp.exp2(l0 - top)
        w1 = jnp.exp2(l1 - top)
        total = w0 + w1
        w0 = w0 / total
        w1 = w1 / total
        lse = top + jnp.log2(total)
        stat = jnp.zeros((TOK, STAT), F32)
        for h in range(GROUP):
            at = slice(h * HD, (h + 1) * HD)
            o_refs[b][:, at] = (
                now[:, at].astype(F32) * w0[:, h : h + 1]
                + before[:, at].astype(F32) * w1[:, h : h + 1]
            ).astype(BF16)
            stat = jnp.where(lax.rem(lanes, GROUP) == h, lse[:, h : h + 1], stat)
        hi, mid, low = split_stat(stat)
        o_refs[b][:, WIDTH:] = jnp.where(
            lanes < GROUP, hi, jnp.where(lanes < 2 * GROUP, mid, low)
        )


def merge(image_range, own, rest, prev):
    whole = lambda shape: pl.BlockSpec(shape, lambda i, t: (0,) * len(shape))
    return pl.pallas_call(
        merge_kernel,
        grid_spec=pltpu.PrefetchScalarGridSpec(
            num_scalar_prefetch=1,
            grid=(1,),
            in_specs=[whole(own.shape), whole(rest.shape), whole(prev.shape)],
            out_specs=[whole((TOK, PACK))] * 4,
        ),
        out_shape=[jax.ShapeDtypeStruct((TOK, PACK), BF16)] * 4,
        compiler_params=params(),
        cost_estimate=pl.CostEstimate(flops=10_000_000, bytes_accessed=4_000_000, transcendentals=0),
        name="merge",
    )(image_range, own, rest, prev)


def finish_kernel(*refs):
    parts, o_ref = refs[:4], refs[4]
    stats = [stat_of(part[...]) for part in parts]
    top = functools.reduce(jnp.maximum, stats)
    weights = [jnp.exp2(s - top) for s in stats]
    total = functools.reduce(jnp.add, weights)
    weights = [w / total for w in weights]
    for h in range(GROUP):
        at = slice(h * HD, (h + 1) * HD)
        o_ref[:, at] = functools.reduce(
            jnp.add,
            [part[:, at].astype(F32) * w[:, h : h + 1] for part, w in zip(parts, weights)],
        ).astype(BF16)


def finish(parts):
    return pl.pallas_call(
        finish_kernel,
        out_shape=jax.ShapeDtypeStruct((TOK, WIDTH), BF16),
        compiler_params=params(),
        cost_estimate=pl.CostEstimate(flops=10_000_000, bytes_accessed=1_500_000, transcendentals=0),
        name="finish",
    )(*parts)


KEY_STEP = 512


def self_kernel(q_ref, near_ref, far_ref, core_near_ref, core_far_ref, o_ref, cache_ref, kv, sems):
    seq = lax.axis_index("seq")
    z = seq // 8
    y = lax.rem(seq // 2, 4)
    core = lax.rem(seq, 2)
    low = z < 2
    low_z = jnp.where(low, z, 3 - z)

    def fetch(slot, when_low, otherwise, half):
        target = kv.at[slot, pl.ds(half * 64, 64)]
        sem = sems.at[slot, half]

        @pl.when(low)
        def _():
            pltpu.make_async_copy(when_low, target, sem).start()

        @pl.when(jnp.logical_not(low))
        def _():
            pltpu.make_async_copy(otherwise, target, sem).start()

    fetch(0, near_ref, far_ref, 0)
    fetch(0, core_near_ref, core_far_ref, 1)
    fetch(1, far_ref, near_ref, 0)
    fetch(1, core_far_ref, core_near_ref, 1)

    def order(z_bit):
        at = lax.broadcasted_iota(jnp.int32, (HD, HD), 1)
        feature = lax.broadcasted_iota(jnp.int32, (HD, HD), 0)
        y_step = (at // 8) % 4
        y_step = y_step ^ (y_step // 2)
        held = (
            ((z_bit ^ ((at // 32) % 2)) * 64)
            + ((y ^ y_step) * 16)
            + ((core ^ (at // 64)) * 8)
            + at % 8
        )
        return (held == feature).astype(BF16)

    key_order = order(low_z)
    value_order = order(1 - low_z)
    parts = 2
    heads = GROUP // parts
    queries = []
    for c in range(parts):
        q = jnp.concatenate(
            [q_ref[:, (c * heads + a) * HD : (c * heads + a + 1) * HD] for a in range(heads)], 0
        )
        queries.append(jnp.dot(q, key_order, preferred_element_type=F32).astype(BF16))
    for slot in range(2):
        for half in range(2):
            pltpu.make_async_copy(
                near_ref, kv.at[slot, pl.ds(half * 64, 64)], sems.at[slot, half]
            ).wait()
    mine = pl.ds(pl.multiple_of(seq * TOK, TOK), TOK)
    for slot, permutation in ((0, key_order), (1, value_order)):
        cache_ref[0, slot * HD : (slot + 1) * HD, :] = jnp.dot(
            permutation, kv[slot, :, mine], preferred_element_type=F32
        ).astype(BF16)
    rows = heads * TOK
    row = lax.rem(lax.broadcasted_iota(jnp.int32, (rows, KEY_STEP), 0), TOK) + seq * TOK
    column = lax.broadcasted_iota(jnp.int32, (rows, KEY_STEP), 1)

    def step(j, states, masked):
        at = pl.ds(pl.multiple_of(j * KEY_STEP, KEY_STEP), KEY_STEP)
        keys = kv[0, :, at]
        values = jnp.concatenate([kv[1, :, at], jnp.ones((HD, KEY_STEP), BF16)], 0)
        out = []
        for c in range(parts):
            m, acc = states[c]
            s = jnp.dot(queries[c], keys, preferred_element_type=F32)
            if masked:
                s = jnp.where(column + j * KEY_STEP <= row, s, NEG)
            new = jnp.maximum(m, jnp.max(s, 1, keepdims=True))
            p = jnp.exp2((s - new) * EXP2_SCALE).astype(BF16)
            acc = acc * jnp.exp2((m - new) * EXP2_SCALE) + lax.dot_general(
                p, values, (((1,), (1,)), ((), ())), preferred_element_type=F32
            )
            out.append((new, acc))
        return tuple(out)

    states = tuple(
        (jnp.full((rows, 1), NEG, F32), jnp.zeros((rows, 2 * HD), F32)) for _ in range(parts)
    )
    full = (seq * TOK) // KEY_STEP
    states = lax.fori_loop(0, full, lambda j, st: step(j, st, False), states)
    states = step(full, states, True)
    for c in range(parts):
        acc = states[c][1]
        out = (acc[:, :HD] * (1.0 / acc[:, HD:])).astype(BF16)
        out = lax.dot_general(
            out, value_order, (((1,), (1,)), ((), ())), preferred_element_type=F32
        ).astype(BF16)
        for a in range(heads):
            h = c * heads + a
            o_ref[:, h * HD : (h + 1) * HD] = out[a * TOK : (a + 1) * TOK]


def self_attend(q, near, far, core_near, core_far):
    tokens = near.shape[1]
    anywhere = pl.BlockSpec(memory_space=pl.ANY)
    return pl.pallas_call(
        self_kernel,
        grid=(1,),
        in_specs=[pl.BlockSpec((TOK, WIDTH), lambda i: (0, 0))] + [anywhere] * 4,
        out_specs=[
            pl.BlockSpec((TOK, WIDTH), lambda i: (0, 0)),
            pl.BlockSpec((1, 2 * HD, TOK), lambda i: (0, 0, 0)),
        ],
        out_shape=[
            jax.ShapeDtypeStruct((TOK, WIDTH), BF16),
            jax.ShapeDtypeStruct((1, 2 * HD, TOK), BF16),
        ],
        scratch_shapes=[
            pltpu.VMEM((2, HD, tokens), BF16),
            pltpu.SemaphoreType.DMA((2, 2)),
        ],
        compiler_params=params(),
        cost_estimate=pl.CostEstimate(
            flops=8 * WIDTH * tokens * HD, bytes_accessed=3_000_000, transcendentals=WIDTH * tokens
        ),
        name="self_attend",
    )(q, near, far, core_near, core_far)


def along_enc(x, by):
    size = lax.axis_size("enc")
    return lax.ppermute(x, "enc", [(i, (i + by) % size) for i in range(size)])


def along_seq(x, target):
    return lax.ppermute(x, "seq", [(i, target(i)) for i in range(lax.axis_size("seq"))])


def on_device(enc_tiles, kv_weight, q_cross, q_self, self_cache, image_range, image_tiles):
    size = lax.axis_size("seq")
    rows = enc_tiles.shape[2]
    q_next = lax.ppermute(q_cross, "seq", [(i + 1, i) for i in range(size - 1)])
    cache = self_cache[0]
    got = along_seq(cache, lambda i: i ^ 2)
    cache = jnp.concatenate([cache, got], 0)
    kv = project(image_tiles, enc_tiles[0, 0], kv_weight, 1664, 832)
    got = along_seq(cache, lambda i: i ^ 6)
    cache = jnp.concatenate([cache, got], 0)
    both = jnp.stack([q_cross, q_next])
    from_far = along_enc(both, 2)
    from_up = along_enc(both, 3)
    from_down = along_enc(both, 1)
    attend = functools.partial(cross, image_tiles, kv=kv, rows=rows, padded=1664)
    own = attend([(q_cross[None], 0)], offsets=(0,))
    got = along_seq(cache, lambda i: i ^ 8)
    near = jnp.concatenate([cache, got], 0)
    far = along_seq(near, lambda i: i ^ 24)
    core_near = along_seq(near, lambda i: i ^ 1)
    following = attend(
        [(q_next[None], 0), (from_up, 1), (from_down, 1), (from_far, 1)],
        offsets=(0, 1, 3, 2),
        last_seq=size - 1,
    )
    previous = lax.ppermute(following, "seq", [(i, i + 1) for i in range(size - 1)])
    core_far = along_seq(far, lambda i: i ^ 1)
    rest = attend([(from_up, 0), (from_down, 0), (from_far, 0)], offsets=(1, 3, 2))
    self_context, cache_seq = self_attend(q_self, near, far, core_near, core_far)
    mine, up, down, far_part = merge(image_range, own, rest, previous)
    parts = [mine, along_enc(far_part, 2), along_enc(up, 1), along_enc(down, 3)]
    return finish(parts), self_context, cache_seq


def solution(mesh):
    return jax.shard_map(
        on_device,
        mesh=mesh,
        in_specs=(
            P("seq", "enc", None, None),
            P(),
            P("seq", "enc"),
            P("seq", "enc"),
            P("enc", "seq", None),
            P("seq", None),
            P(),
        ),
        out_specs=(P("seq", "enc"), P("seq", "enc"), P("enc", None, "seq")),
        check_vma=False,
    )
```

```python
import functools
import math

import jax
import jax.numpy as jnp
from jax import lax
from jax.experimental import pallas as pl
from jax.experimental.pallas import tpu as pltpu
from jax.sharding import PartitionSpec as P

HD = 128
GROUP = 8
TOK = 128
WIDTH = GROUP * HD
STAT = 128
PACK = WIDTH + STAT
NEG = -1e30
EXP2_SCALE = math.log2(math.e) / math.sqrt(HD)
VMEM = 28 * 1024 * 1024
BF16 = jnp.bfloat16
F32 = jnp.float32
COST_UNIT = 1_150_000_000


def cost(microseconds):
    return pl.CostEstimate(
        flops=int(microseconds * COST_UNIT), bytes_accessed=1000, transcendentals=0
    )


def params(limit=VMEM):
    return pltpu.CompilerParams(vmem_limit_bytes=limit)


def stage_kernel(x_hbm, w_hbm, _, x_ref, w_ref, sems):
    copies = [
        pltpu.make_async_copy(x_hbm, x_ref, sems.at[0]),
        pltpu.make_async_copy(w_hbm, w_ref, sems.at[1]),
    ]
    for copy in copies:
        copy.start()
    for copy in copies:
        copy.wait()


def stage(x, w, after):
    anywhere = pl.BlockSpec(memory_space=pl.ANY)
    in_vmem = pl.BlockSpec(memory_space=pltpu.VMEM)
    return pl.pallas_call(
        stage_kernel,
        in_specs=[anywhere] * 3,
        out_specs=[in_vmem] * 2,
        out_shape=[jax.ShapeDtypeStruct(x.shape, BF16), jax.ShapeDtypeStruct(w.shape, BF16)],
        scratch_shapes=[pltpu.SemaphoreType.DMA((2,))],
        compiler_params=params(),
        cost_estimate=cost(4),
        name="stage",
    )(x, w, after)


def project_kernel(tiles_ref, x_ref, w_ref, *refs, offsets, step):
    o_refs = refs[-len(offsets) :]
    enc = lax.axis_index("enc")
    live = enc < tiles_ref[lax.axis_index("seq")]
    rows = x_ref.shape[0]
    sent = o_refs[0].shape[1]

    @pl.when(live)
    def _():
        for o_ref, group in zip(o_refs, offsets):
            for b, offset in enumerate(group):
                g = lax.rem(enc + offset, 4)
                w = w_ref[:, pl.ds(pl.multiple_of(g * 2 * HD, 2 * HD), 2 * HD)]
                for start in range(0, rows, step):
                    end = min(start + step, rows)
                    y = jnp.dot(x_ref[start:end], w, preferred_element_type=F32)
                    if end == rows:
                        y = jnp.concatenate([y, jnp.zeros((sent - rows, 2 * HD), F32)], 0)
                        end = sent
                    o_ref[b, start:end] = y.astype(BF16)


def project(tiles, x, w, after, offsets, sent, step):
    in_vmem = pl.BlockSpec(memory_space=pltpu.VMEM)
    return pl.pallas_call(
        functools.partial(project_kernel, offsets=offsets, step=step),
        in_specs=[pl.BlockSpec(memory_space=pltpu.SMEM), in_vmem, in_vmem]
        + [pl.BlockSpec(memory_space=pl.ANY)] * len(after),
        out_specs=[in_vmem for _ in offsets],
        out_shape=[jax.ShapeDtypeStruct((len(o), sent, 2 * HD), BF16) for o in offsets],
        compiler_params=params(),
        cost_estimate=cost(5.5),
        name="project",
    )(tiles, x, w, *after)


def split_stat(lse):
    hi = lse.astype(BF16)
    rest = lse - hi.astype(F32)
    mid = rest.astype(BF16)
    low = (rest - mid.astype(F32)).astype(BF16)
    return hi, mid, low


def cross_kernel(tiles_ref, range_ref, *refs, waits, count, picks, priors, outputs, rows, last):
    refs = refs[waits:]
    q_refs = refs[:count]
    kv_ref = refs[count]
    prior_ref = refs[count + 1] if priors else None
    o_refs = refs[-3 - outputs : -3]
    queries, kv, sems = refs[-3:]
    sent = kv_ref.shape[1]
    padded = kv.shape[1]
    seq = lax.axis_index("seq")
    live = lax.axis_index("enc") < tiles_ref[seq]
    each = count // outputs
    lanes = lax.broadcasted_iota(jnp.int32, (1, HD), 1)

    def sees(image, shape):
        spans = [
            ((range_ref[c, 0] <= image) & (image < range_ref[c, 1])).astype(jnp.int32)
            for c in range(2)
        ]
        token = lax.rem(lax.broadcasted_iota(jnp.int32, shape, 0), TOK)
        return jnp.where(token < TOK // 2, spans[0], spans[1]) != 0

    if not priors:
        live = live & (seq < last)

    @pl.when(jnp.logical_not(live))
    def _():
        for b in range(count):
            o_ref = o_refs[b // each]
            if priors:
                o_ref[b % each, :, :WIDTH] = prior_ref[priors[b], :, :WIDTH]
                o_ref[b % each, :, WIDTH:] = jnp.where(
                    sees(seq - 1, (TOK, STAT)), prior_ref[priors[b], :, WIDTH:].astype(F32), NEG
                ).astype(BF16)
            else:
                o_ref[b % each, :, :WIDTH] = jnp.zeros((TOK, WIDTH), BF16)
                o_ref[b % each, :, WIDTH:] = jnp.full((TOK, STAT), NEG, BF16)

    @pl.when(live)
    def _():
        def fetch(b):
            return pltpu.make_async_copy(
                kv_ref.at[picks[b]], kv.at[b, pl.ds(0, sent)], sems.at[b]
            )

        for b in range(count):
            fetch(b).start()
        for b in range(count):
            kv[b, sent:] = jnp.zeros((padded - sent, 2 * HD), BF16)
            for h in range(GROUP):
                queries[b, h * TOK : (h + 1) * TOK] = q_refs[b][0, :, h * HD : (h + 1) * HD]
        edge = jnp.where(lanes < rows - (padded - HD), 0.0, NEG)
        part = 4
        if priors:
            seen = sees(seq, (part * TOK, 1))
            seen_before = sees(seq - 1, (TOK, GROUP))

        for b in range(count):
            fetch(b).wait()
            o_ref, at_out = o_refs[b // each], b % each
            keys = kv[b, :, :HD]
            values = jnp.concatenate([kv[b, :, HD:], jnp.ones((padded, HD), BF16)], 1)
            if priors:
                before = jnp.where(seen_before, stat_of(prior_ref[priors[b]]), NEG)
            tops = jnp.zeros((TOK, STAT), F32)
            sums = jnp.ones((TOK, STAT), F32)
            for c in range(GROUP // part):
                q = queries[b, c * part * TOK : (c + 1) * part * TOK]
                s = lax.dot_general(q, keys, (((1,), (1,)), ((), ())), preferred_element_type=F32)
                s = jnp.concatenate([s[:, : padded - HD], s[:, padded - HD :] + edge], 1)
                m = jnp.max(s, 1, keepdims=True) * EXP2_SCALE
                if priors:
                    prior = jnp.concatenate(
                        [before[:, c * part + a : c * part + a + 1] for a in range(part)], 0
                    )
                    m = jnp.where(seen, jnp.maximum(m, prior), prior)
                p = jnp.exp2(s * EXP2_SCALE - m).astype(BF16)
                mixed = jnp.dot(p, values, preferred_element_type=F32)
                total = mixed[:, HD:]
                mixed = mixed[:, :HD]
                if priors:
                    share = jnp.exp2(prior - m)
                    total = jnp.where(seen, total, 0.0) + share
                    out = jnp.concatenate(
                        [
                            prior_ref[priors[b], :, (c * part + a) * HD : (c * part + a + 1) * HD]
                            for a in range(part)
                        ],
                        0,
                    ).astype(F32)
                    mixed = jnp.where(seen, mixed, 0.0) + out * share
                out = (mixed * (1.0 / total)).astype(BF16)
                for a in range(part):
                    h = c * part + a
                    at = slice(a * TOK, (a + 1) * TOK)
                    o_ref[at_out, :, h * HD : (h + 1) * HD] = out[at]
                    here = lax.rem(lanes, GROUP) == h
                    tops = jnp.where(here, m[at], tops)
                    sums = jnp.where(here, total[at], sums)
            hi, mid, low = split_stat(tops + jnp.log2(sums))
            o_ref[at_out, :, WIDTH:] = jnp.where(
                lanes < GROUP, hi, jnp.where(lanes < 2 * GROUP, mid, low)
            )


def cross(tiles, image_range, queries, kv, picks, rows, prior=None, priors=(), outputs=1, after=()):
    count = len(queries)
    sent = kv.shape[1]
    padded = -(-rows // HD) * HD
    each = count // outputs
    whole = lambda shape: pl.BlockSpec(shape, lambda i, t, r: (0,) * len(shape))
    return pl.pallas_call(
        functools.partial(
            cross_kernel,
            waits=len(after),
            count=count,
            picks=picks,
            priors=priors,
            outputs=outputs,
            rows=rows,
            last=lax.axis_size("seq") - 1,
        ),
        grid_spec=pltpu.PrefetchScalarGridSpec(
            num_scalar_prefetch=2,
            grid=(1,),
            in_specs=[pl.BlockSpec(memory_space=pl.ANY)] * len(after)
            + [
                pl.BlockSpec((1, TOK, WIDTH), functools.partial(lambda k, i, t, r: (k, 0, 0), k))
                for _, k in queries
            ]
            + [pl.BlockSpec(memory_space=pl.ANY)]
            + ([whole(prior.shape)] if priors else []),
            out_specs=[whole((each, TOK, PACK))] * outputs,
            scratch_shapes=[
                pltpu.VMEM((count, GROUP * TOK, HD), BF16),
                pltpu.VMEM((count, padded, 2 * HD), BF16),
                pltpu.SemaphoreType.DMA((count,)),
            ],
        ),
        out_shape=[jax.ShapeDtypeStruct((each, TOK, PACK), BF16)] * outputs,
        compiler_params=params(),
        cost_estimate=cost(2.9 * count),
        name="cross",
    )(
        tiles,
        image_range,
        *after,
        *[q if q.ndim == 3 else q[None] for q, _ in queries],
        kv,
        *([prior] if priors else []),
    )


def stat_of(packed):
    s = packed[:, WIDTH:].astype(F32)
    return s[:, :GROUP] + s[:, GROUP : 2 * GROUP] + s[:, 2 * GROUP : 3 * GROUP]


def finish_kernel(*refs):
    parts, o_ref = refs[:4], refs[4]
    stats = [stat_of(part[0]) for part in parts]
    top = functools.reduce(jnp.maximum, stats)
    weights = [jnp.exp2(s - top) for s in stats]
    total = functools.reduce(jnp.add, weights)
    weights = [w / total for w in weights]
    for h in range(GROUP):
        at = slice(h * HD, (h + 1) * HD)
        o_ref[:, at] = functools.reduce(
            jnp.add,
            [part[0, :, at].astype(F32) * w[:, h : h + 1] for part, w in zip(parts, weights)],
        ).astype(BF16)


def finish(parts):
    return pl.pallas_call(
        finish_kernel,
        out_shape=jax.ShapeDtypeStruct((TOK, WIDTH), BF16),
        compiler_params=params(),
        cost_estimate=cost(1.5),
        name="finish",
    )(*parts)


KEY_STEP = 1024


def self_kernel(q_ref, near_ref, far_ref, core_near_ref, core_far_ref, _, o_ref, cache_ref, kv, sems):
    seq = lax.axis_index("seq")
    z = seq // 8
    y = lax.rem(seq // 2, 4)
    core = lax.rem(seq, 2)
    low = z < 2
    low_z = jnp.where(low, z, 3 - z)

    def fetch(slot, when_low, otherwise, half):
        target = kv.at[slot, pl.ds(half * 64, 64)]
        sem = sems.at[slot, half]

        @pl.when(low)
        def _():
            pltpu.make_async_copy(when_low, target, sem).start()

        @pl.when(jnp.logical_not(low))
        def _():
            pltpu.make_async_copy(otherwise, target, sem).start()

    fetch(0, near_ref, far_ref, 0)
    fetch(0, core_near_ref, core_far_ref, 1)
    fetch(1, far_ref, near_ref, 0)
    fetch(1, core_far_ref, core_near_ref, 1)

    def order(z_bit):
        at = lax.broadcasted_iota(jnp.int32, (HD, HD), 1)
        feature = lax.broadcasted_iota(jnp.int32, (HD, HD), 0)
        y_step = (at // 8) % 4
        y_step = y_step ^ (y_step // 2)
        held = (
            ((z_bit ^ ((at // 32) % 2)) * 64)
            + ((y ^ y_step) * 16)
            + ((core ^ (at // 64)) * 8)
            + at % 8
        )
        return (held == feature).astype(BF16)

    key_order = order(low_z)
    value_order = order(1 - low_z)
    parts = 2
    heads = GROUP // parts
    queries = []
    for c in range(parts):
        q = jnp.concatenate(
            [q_ref[:, (c * heads + a) * HD : (c * heads + a + 1) * HD] for a in range(heads)], 0
        )
        queries.append(jnp.dot(q, key_order, preferred_element_type=F32).astype(BF16))
    for slot in range(2):
        for half in range(2):
            pltpu.make_async_copy(
                near_ref, kv.at[slot, pl.ds(half * 64, 64)], sems.at[slot, half]
            ).wait()
    mine = pl.ds(pl.multiple_of(seq * TOK, TOK), TOK)
    for slot, permutation in ((0, key_order), (1, value_order)):
        cache_ref[0, slot * HD : (slot + 1) * HD, :] = jnp.dot(
            permutation, kv[slot, :, mine], preferred_element_type=F32
        ).astype(BF16)
    rows = heads * TOK
    row = lax.rem(lax.broadcasted_iota(jnp.int32, (rows, KEY_STEP), 0), TOK) + seq * TOK
    column = lax.broadcasted_iota(jnp.int32, (rows, KEY_STEP), 1)

    def step(j, states, masked):
        at = pl.ds(pl.multiple_of(j * KEY_STEP, KEY_STEP), KEY_STEP)
        keys = kv[0, :, at]
        values = jnp.concatenate([kv[1, :, at], jnp.ones((HD, KEY_STEP), BF16)], 0)
        out = []
        for c in range(parts):
            m, acc = states[c]
            s = jnp.dot(queries[c], keys, preferred_element_type=F32)
            if masked:
                s = jnp.where(column + j * KEY_STEP <= row, s, NEG)
            new = jnp.maximum(m, jnp.max(s, 1, keepdims=True))
            p = jnp.exp2((s - new) * EXP2_SCALE).astype(BF16)
            acc = acc * jnp.exp2((m - new) * EXP2_SCALE) + lax.dot_general(
                p, values, (((1,), (1,)), ((), ())), preferred_element_type=F32
            )
            out.append((new, acc))
        return tuple(out)

    states = tuple(
        (jnp.full((rows, 1), NEG, F32), jnp.zeros((rows, 2 * HD), F32)) for _ in range(parts)
    )
    full = (seq * TOK) // KEY_STEP
    states = lax.fori_loop(0, full, lambda j, st: step(j, st, False), states)
    states = step(full, states, True)
    for c in range(parts):
        acc = states[c][1]
        out = (acc[:, :HD] * (1.0 / acc[:, HD:])).astype(BF16)
        out = lax.dot_general(
            out, value_order, (((1,), (1,)), ((), ())), preferred_element_type=F32
        ).astype(BF16)
        for a in range(heads):
            h = c * heads + a
            o_ref[:, h * HD : (h + 1) * HD] = out[a * TOK : (a + 1) * TOK]


def self_attend(q, near, far, core_near, core_far, after):
    tokens = near.shape[1]
    anywhere = pl.BlockSpec(memory_space=pl.ANY)
    return pl.pallas_call(
        self_kernel,
        grid=(1,),
        in_specs=[pl.BlockSpec((TOK, WIDTH), lambda i: (0, 0))] + [anywhere] * 5,
        out_specs=[
            pl.BlockSpec((TOK, WIDTH), lambda i: (0, 0)),
            pl.BlockSpec((1, 2 * HD, TOK), lambda i: (0, 0, 0)),
        ],
        out_shape=[
            jax.ShapeDtypeStruct((TOK, WIDTH), BF16),
            jax.ShapeDtypeStruct((1, 2 * HD, TOK), BF16),
        ],
        scratch_shapes=[
            pltpu.VMEM((2, HD, tokens), BF16),
            pltpu.SemaphoreType.DMA((2, 2)),
        ],
        compiler_params=params(),
        cost_estimate=cost(6),
        name="self_attend",
    )(q, near, far, core_near, core_far, after)


def along_enc(x, by):
    size = lax.axis_size("enc")
    return lax.ppermute(x, "enc", [(i, (i + by) % size) for i in range(size)])


def along_seq(x, target):
    return lax.ppermute(x, "seq", [(i, target(i)) for i in range(lax.axis_size("seq"))])


def tied(x, *others):
    return lax.optimization_barrier((x, *others))[0]


def on_device(enc_tiles, kv_weight, q_cross, q_self, self_cache, image_range, image_tiles):
    rows = enc_tiles.shape[2]
    sent = -(-rows // 16) * 16
    size = lax.axis_size("seq")
    forward = lambda x: lax.ppermute(x, "seq", [(i, i + 1) for i in range(size - 1)])
    backward = lambda x: lax.ppermute(x, "seq", [(i + 1, i) for i in range(size - 1)])
    cache = self_cache[0]
    got = along_seq(cache, lambda i: i ^ 2)
    q_far = along_enc(q_cross, 2)
    q_up = along_enc(q_cross, 3)
    q_down = along_enc(q_cross, 1)
    q_next = backward(q_cross)
    cache = jnp.concatenate([cache, got], 0)
    tiles, weights = stage(enc_tiles[0, 0], kv_weight, cache)
    got = along_seq(cache, lambda i: i ^ 6)
    cache = jnp.concatenate([cache, tied(got, tiles)], 0)
    got = along_seq(cache, lambda i: i ^ 8)
    q_rest = jnp.stack([q_up, q_down, q_far])
    q_rest_next = backward(q_rest)
    (kv,) = project(
        image_tiles, tiles, weights, (cache, q_rest, q_next), ((0, 1, 3, 2),), sent, 416
    )
    near_cache = jnp.concatenate([cache, tied(got, kv)], 0)
    far_cache = along_seq(near_cache, lambda i: i ^ 24)
    core_near = along_seq(near_cache, lambda i: i ^ 1)
    attend = functools.partial(cross, image_tiles, image_range, kv=kv, rows=rows)
    (following,) = attend(
        [(q_next, 0), (q_rest_next, 0), (q_rest_next, 1), (q_rest_next, 2)],
        picks=(0, 1, 2, 3),
        after=(near_cache,),
    )
    prior = forward(following)
    core_far = along_seq(tied(far_cache, following), lambda i: i ^ 1)
    self_context, cache_seq = self_attend(
        q_self, near_cache, far_cache, core_near, core_far, following
    )
    (far,) = attend([(q_rest, 2)], picks=(3,), prior=prior, priors=(3,), after=(cache_seq,))
    far_got = along_enc(far, 2)
    up, down = attend(
        [(q_rest, 0), (q_rest, 1)],
        picks=(1, 2),
        prior=prior,
        priors=(1, 2),
        outputs=2,
        after=(far,),
    )
    up_got = along_enc(up, 1)
    down_got = along_enc(down, 3)
    (mine,) = attend([(q_cross, 0)], picks=(0,), prior=prior, priors=(0,), after=(up,))
    return finish([mine, far_got, up_got, down_got]), self_context, cache_seq


def solution(mesh):
    return jax.shard_map(
        on_device,
        mesh=mesh,
        in_specs=(
            P("seq", "enc", None, None),
            P(),
            P("seq", "enc"),
            P("seq", "enc"),
            P("enc", "seq", None),
            P("seq", None),
            P(),
        ),
        out_specs=(P("seq", "enc"), P("seq", "enc"), P("enc", None, "seq")),
        check_vma=False,
    )
```

```python
import functools
import math

import jax
import jax.numpy as jnp
from jax import lax
from jax.experimental import pallas as pl
from jax.experimental.pallas import tpu as pltpu
from jax.sharding import PartitionSpec as P

HD = 128
GROUP = 8
TOK = 128
WIDTH = GROUP * HD
STAT = 128
PACK = WIDTH + STAT
NEG = -1e30
EXP2_SCALE = math.log2(math.e) / math.sqrt(HD)
VMEM = 28 * 1024 * 1024
BF16 = jnp.bfloat16
F32 = jnp.float32
COST_UNIT = 1_150_000_000


def cost(microseconds):
    return pl.CostEstimate(
        flops=int(microseconds * COST_UNIT), bytes_accessed=1000, transcendentals=0
    )


def params(limit=VMEM):
    return pltpu.CompilerParams(vmem_limit_bytes=limit)


def stage_kernel(x_hbm, w_hbm, _, x_ref, w_ref, sems):
    copies = [
        pltpu.make_async_copy(x_hbm, x_ref, sems.at[0]),
        pltpu.make_async_copy(w_hbm, w_ref, sems.at[1]),
    ]
    for copy in copies:
        copy.start()
    for copy in copies:
        copy.wait()


def stage(x, w, after):
    anywhere = pl.BlockSpec(memory_space=pl.ANY)
    in_vmem = pl.BlockSpec(memory_space=pltpu.VMEM)
    return pl.pallas_call(
        stage_kernel,
        in_specs=[anywhere] * 3,
        out_specs=[in_vmem] * 2,
        out_shape=[jax.ShapeDtypeStruct(x.shape, BF16), jax.ShapeDtypeStruct(w.shape, BF16)],
        scratch_shapes=[pltpu.SemaphoreType.DMA((2,))],
        compiler_params=params(),
        cost_estimate=cost(4),
        name="stage",
    )(x, w, after)


def project_kernel(tiles_ref, x_ref, w_ref, *refs, offsets, step):
    o_refs = refs[-len(offsets) :]
    enc = lax.axis_index("enc")
    live = enc < tiles_ref[lax.axis_index("seq")]
    rows = x_ref.shape[0]
    sent = o_refs[0].shape[1]

    @pl.when(live)
    def _():
        for o_ref, group in zip(o_refs, offsets):
            for b, offset in enumerate(group):
                g = lax.rem(enc + offset, 4)
                w = w_ref[:, pl.ds(pl.multiple_of(g * 2 * HD, 2 * HD), 2 * HD)]
                for start in range(0, rows, step):
                    end = min(start + step, rows)
                    y = jnp.dot(x_ref[start:end], w, preferred_element_type=F32)
                    if end == rows:
                        y = jnp.concatenate([y, jnp.zeros((sent - rows, 2 * HD), F32)], 0)
                        end = sent
                    o_ref[b, start:end] = y.astype(BF16)


def project(tiles, x, w, after, offsets, sent, step):
    in_vmem = pl.BlockSpec(memory_space=pltpu.VMEM)
    return pl.pallas_call(
        functools.partial(project_kernel, offsets=offsets, step=step),
        in_specs=[pl.BlockSpec(memory_space=pltpu.SMEM), in_vmem, in_vmem]
        + [pl.BlockSpec(memory_space=pl.ANY)] * len(after),
        out_specs=[in_vmem for _ in offsets],
        out_shape=[jax.ShapeDtypeStruct((len(o), sent, 2 * HD), BF16) for o in offsets],
        compiler_params=params(),
        cost_estimate=cost(5.5),
        name="project",
    )(tiles, x, w, *after)


def split_stat(lse):
    hi = lse.astype(BF16)
    rest = lse - hi.astype(F32)
    mid = rest.astype(BF16)
    low = (rest - mid.astype(F32)).astype(BF16)
    return hi, mid, low


def cross_kernel(tiles_ref, range_ref, *refs, waits, count, picks, priors, outputs, rows, last, carried):
    carry_ref = refs[waits - 1] if carried else None
    refs = refs[waits:]
    q_refs = refs[:count]
    kv_ref = refs[count]
    prior_ref = refs[count + 1] if priors else None
    o_refs = refs[-1 - outputs : -1]
    queries = refs[-1]
    padded = kv_ref.shape[1]
    seq = lax.axis_index("seq")
    live = lax.axis_index("enc") < tiles_ref[seq]
    each = (count + carried) // outputs
    if carried:
        o_refs[0][:carried] = carry_ref[...]
    lanes = lax.broadcasted_iota(jnp.int32, (1, HD), 1)

    def sees(image, shape):
        spans = [
            ((range_ref[c, 0] <= image) & (image < range_ref[c, 1])).astype(jnp.int32)
            for c in range(2)
        ]
        token = lax.rem(lax.broadcasted_iota(jnp.int32, shape, 0), TOK)
        return jnp.where(token < TOK // 2, spans[0], spans[1]) != 0

    if not priors:
        live = live & (seq < last)

    @pl.when(jnp.logical_not(live))
    def _():
        for b in range(count):
            o_ref = o_refs[b // each]
            if priors:
                o_ref[b % each, :, :WIDTH] = prior_ref[priors[b], :, :WIDTH]
                o_ref[b % each, :, WIDTH:] = jnp.where(
                    sees(seq - 1, (TOK, STAT)), prior_ref[priors[b], :, WIDTH:].astype(F32), NEG
                ).astype(BF16)
            else:
                o_ref[b + carried, :, :WIDTH] = jnp.zeros((TOK, WIDTH), BF16)
                o_ref[b + carried, :, WIDTH:] = jnp.full((TOK, STAT), NEG, BF16)

    @pl.when(live)
    def _():
        for b in range(count):
            for h in range(GROUP):
                queries[b, h * TOK : (h + 1) * TOK] = q_refs[b][0, :, h * HD : (h + 1) * HD]
        edge = jnp.where(lanes < rows - (padded - HD), 0.0, NEG)
        part = 4
        if priors:
            seen = sees(seq, (part * TOK, 1))
            seen_before = sees(seq - 1, (TOK, GROUP))

        for b in range(count):
            o_ref, at_out = o_refs[(b + carried) // each], (b + carried) % each
            keys = kv_ref[picks[b], :, :HD]
            values = jnp.concatenate([kv_ref[picks[b], :, HD:], jnp.ones((padded, HD), BF16)], 1)
            if priors:
                before = jnp.where(seen_before, stat_of(prior_ref[priors[b]]), NEG)
            tops = jnp.zeros((TOK, STAT), F32)
            sums = jnp.ones((TOK, STAT), F32)
            for c in range(GROUP // part):
                q = queries[b, c * part * TOK : (c + 1) * part * TOK]
                s = lax.dot_general(q, keys, (((1,), (1,)), ((), ())), preferred_element_type=F32)
                s = jnp.concatenate([s[:, : padded - HD], s[:, padded - HD :] + edge], 1)
                m = jnp.max(s, 1, keepdims=True) * EXP2_SCALE
                if priors:
                    prior = jnp.concatenate(
                        [before[:, c * part + a : c * part + a + 1] for a in range(part)], 0
                    )
                    m = jnp.where(seen, jnp.maximum(m, prior), prior)
                p = jnp.exp2(s * EXP2_SCALE - m).astype(BF16)
                mixed = jnp.dot(p, values, preferred_element_type=F32)
                total = mixed[:, HD:]
                mixed = mixed[:, :HD]
                if priors:
                    share = jnp.exp2(prior - m)
                    total = jnp.where(seen, total, 0.0) + share
                    out = jnp.concatenate(
                        [
                            prior_ref[priors[b], :, (c * part + a) * HD : (c * part + a + 1) * HD]
                            for a in range(part)
                        ],
                        0,
                    ).astype(F32)
                    mixed = jnp.where(seen, mixed, 0.0) + out * share
                out = (mixed * (1.0 / total)).astype(BF16)
                for a in range(part):
                    h = c * part + a
                    at = slice(a * TOK, (a + 1) * TOK)
                    o_ref[at_out, :, h * HD : (h + 1) * HD] = out[at]
                    here = lax.rem(lanes, GROUP) == h
                    tops = jnp.where(here, m[at], tops)
                    sums = jnp.where(here, total[at], sums)
            hi, mid, low = split_stat(tops + jnp.log2(sums))
            o_ref[at_out, :, WIDTH:] = jnp.where(
                lanes < GROUP, hi, jnp.where(lanes < 2 * GROUP, mid, low)
            )


def cross(tiles, image_range, queries, kv, picks, rows, prior=None, priors=(), outputs=1, after=(), carry=None, last=None):
    count = len(queries)
    carried = 0 if carry is None else carry.shape[0]
    each = (count + carried) // outputs
    whole = lambda shape: pl.BlockSpec(shape, lambda i, t, r: (0,) * len(shape))
    return pl.pallas_call(
        functools.partial(
            cross_kernel,
            waits=len(after) + min(carried, 1),
            carried=carried,
            count=count,
            picks=picks,
            priors=priors,
            outputs=outputs,
            rows=rows,
            last=lax.axis_size("seq") if last is None else last,
        ),
        grid_spec=pltpu.PrefetchScalarGridSpec(
            num_scalar_prefetch=2,
            grid=(1,),
            in_specs=[pl.BlockSpec(memory_space=pl.ANY)] * len(after)
            + ([whole(carry.shape)] if carried else [])
            + [
                pl.BlockSpec((1, TOK, WIDTH), functools.partial(lambda k, i, t, r: (k, 0, 0), k))
                for _, k in queries
            ]
            + [pl.BlockSpec(memory_space=pltpu.VMEM)]
            + ([whole(prior.shape)] if priors else []),
            out_specs=[whole((each, TOK, PACK))] * outputs,
            scratch_shapes=[pltpu.VMEM((count, GROUP * TOK, HD), BF16)],
        ),
        out_shape=[jax.ShapeDtypeStruct((each, TOK, PACK), BF16)] * outputs,
        compiler_params=params(),
        cost_estimate=cost(2.9 * count),
        name="cross",
    )(
        tiles,
        image_range,
        *after,
        *([carry] if carried else []),
        *[q if q.ndim == 3 else q[None] for q, _ in queries],
        kv,
        *([prior] if priors else []),
    )


def stat_of(packed):
    s = packed[:, WIDTH:].astype(F32)
    return s[:, :GROUP] + s[:, GROUP : 2 * GROUP] + s[:, 2 * GROUP : 3 * GROUP]


def merge_kernel(range_ref, now_ref, prior_ref, *o_refs, picks):
    seq = lax.axis_index("seq")
    first = lax.broadcasted_iota(jnp.int32, (TOK, GROUP), 0) < TOK // 2
    seen = []
    for image in (seq, seq - 1):
        spans = [
            ((range_ref[c, 0] <= image) & (image < range_ref[c, 1])).astype(jnp.int32)
            for c in range(2)
        ]
        seen.append(jnp.where(first, spans[0], spans[1]) != 0)
    lanes = lax.broadcasted_iota(jnp.int32, (1, STAT), 1)
    for b, (pick, o_ref) in enumerate(zip(picks, o_refs)):
        l0 = jnp.where(seen[0], stat_of(now_ref[b]), NEG)
        l1 = jnp.where(seen[1], stat_of(prior_ref[pick]), NEG)
        top = jnp.maximum(l0, l1)
        w0 = jnp.exp2(l0 - top)
        w1 = jnp.exp2(l1 - top)
        total = w0 + w1
        scale = 1.0 / total
        w0 = w0 * scale
        w1 = w1 * scale
        hi, mid, low = split_stat(top + jnp.log2(total))
        o_ref[0, :, WIDTH:] = jnp.concatenate(
            [hi, mid, low, jnp.zeros((TOK, STAT - 3 * GROUP), BF16)], 1
        )
        for h in range(GROUP):
            at = slice(h * HD, (h + 1) * HD)
            o_ref[0, :, at] = (
                now_ref[b, :, at].astype(F32) * w0[:, h : h + 1]
                + prior_ref[pick, :, at].astype(F32) * w1[:, h : h + 1]
            ).astype(BF16)


def merge(image_range, now, prior, picks, after):
    in_vmem = pl.BlockSpec(memory_space=pltpu.VMEM)

    def kernel(range_ref, _, *refs):
        merge_kernel(range_ref, *refs, picks=picks)

    return pl.pallas_call(
        kernel,
        in_specs=[
            pl.BlockSpec(memory_space=pltpu.SMEM),
            pl.BlockSpec(memory_space=pl.ANY),
            in_vmem,
            in_vmem,
        ],
        out_specs=[in_vmem] * len(picks),
        out_shape=[jax.ShapeDtypeStruct((1, TOK, PACK), BF16)] * len(picks),
        compiler_params=params(),
        cost_estimate=cost(2),
        name="merge",
    )(image_range, after, now, prior)


def finish_kernel(*refs):
    parts, o_ref = refs[:4], refs[5]
    stats = [stat_of(part[0]) for part in parts]
    top = functools.reduce(jnp.maximum, stats)
    weights = [jnp.exp2(s - top) for s in stats]
    total = functools.reduce(jnp.add, weights)
    weights = [w / total for w in weights]
    for h in range(GROUP):
        at = slice(h * HD, (h + 1) * HD)
        o_ref[:, at] = functools.reduce(
            jnp.add,
            [part[0, :, at].astype(F32) * w[:, h : h + 1] for part, w in zip(parts, weights)],
        ).astype(BF16)


def finish(parts, after):
    return pl.pallas_call(
        finish_kernel,
        in_specs=[pl.BlockSpec(memory_space=pltpu.VMEM)] * 4 + [pl.BlockSpec(memory_space=pl.ANY)],
        out_specs=pl.BlockSpec(memory_space=pltpu.VMEM),
        out_shape=jax.ShapeDtypeStruct((TOK, WIDTH), BF16),
        compiler_params=params(),
        cost_estimate=cost(1.5),
        name="finish",
    )(*parts, after)


KEY_STEP = 2048


def self_kernel(q_ref, near, far, core_near, core_far, _, o_ref, cache_ref, mark_ref):
    mark_ref[...] = jnp.zeros(mark_ref.shape, F32)
    low = lax.axis_index("seq") < lax.axis_size("seq") // 2

    @pl.when(low)
    def _():
        self_body(q_ref, near, core_near, far, core_far, o_ref, cache_ref, True)

    @pl.when(jnp.logical_not(low))
    def _():
        self_body(q_ref, far, core_far, near, core_near, o_ref, cache_ref, False)


def self_body(q_ref, key_here, key_core, value_here, value_core, o_ref, cache_ref, low):
    seq = lax.axis_index("seq")
    z = seq // 8
    y = lax.rem(seq // 2, 4)
    core = lax.rem(seq, 2)
    low_z = z if low else 3 - z

    def order(z_bit):
        at = lax.broadcasted_iota(jnp.int32, (HD, HD), 1)
        feature = lax.broadcasted_iota(jnp.int32, (HD, HD), 0)
        y_step = (at // 8) % 4
        y_step = y_step ^ (y_step // 2)
        held = (
            ((z_bit ^ ((at // 32) % 2)) * 64)
            + ((y ^ y_step) * 16)
            + ((core ^ (at // 64)) * 8)
            + at % 8
        )
        return (held == feature).astype(BF16)

    key_order = order(low_z)
    value_order = order(1 - low_z)

    def keys_at(at):
        return jnp.concatenate([key_here[:, at], key_core[:, at]], 0)

    def values_at(at):
        return jnp.concatenate([value_here[:, at], value_core[:, at]], 0)

    parts = 2
    heads = GROUP // parts
    queries = []
    for c in range(parts):
        q = jnp.concatenate(
            [q_ref[:, (c * heads + a) * HD : (c * heads + a + 1) * HD] for a in range(heads)], 0
        )
        queries.append(jnp.dot(q, key_order, preferred_element_type=F32).astype(BF16))
    mine = pl.ds(pl.multiple_of(seq * TOK, TOK), TOK)
    for slot, permutation, held in ((0, key_order, keys_at), (1, value_order, values_at)):
        cache_ref[0, slot * HD : (slot + 1) * HD, :] = jnp.dot(
            permutation, held(mine), preferred_element_type=F32
        ).astype(BF16)
    rows = heads * TOK

    def step(j, states, masked):
        at = pl.ds(pl.multiple_of(j * KEY_STEP, KEY_STEP), KEY_STEP)
        keys = keys_at(at)
        values = jnp.concatenate([values_at(at), jnp.ones((HD, KEY_STEP), BF16)], 0)
        if masked:
            row = lax.rem(lax.broadcasted_iota(jnp.int32, (rows, KEY_STEP), 0), TOK) + seq * TOK
            allowed = lax.broadcasted_iota(jnp.int32, (rows, KEY_STEP), 1) + j * KEY_STEP <= row
        out = []
        for c in range(parts):
            m, acc = states[c]
            s = jnp.dot(queries[c], keys, preferred_element_type=F32)
            if masked:
                s = jnp.where(allowed, s, NEG)
            new = jnp.maximum(m, jnp.max(s, 1, keepdims=True))
            p = jnp.exp2((s - new) * EXP2_SCALE).astype(BF16)
            acc = acc * jnp.exp2((m - new) * EXP2_SCALE) + lax.dot_general(
                p, values, (((1,), (1,)), ((), ())), preferred_element_type=F32
            )
            out.append((new, acc))
        return tuple(out)

    states = tuple(
        (jnp.full((rows, 1), NEG, F32), jnp.zeros((rows, 2 * HD), F32)) for _ in range(parts)
    )
    full = (seq * TOK) // KEY_STEP
    states = lax.fori_loop(0, full, lambda j, st: step(j, st, False), states)
    states = step(full, states, True)
    for c in range(parts):
        acc = states[c][1]
        out = (acc[:, :HD] * (1.0 / acc[:, HD:])).astype(BF16)
        out = lax.dot_general(
            out, value_order, (((1,), (1,)), ((), ())), preferred_element_type=F32
        ).astype(BF16)
        for a in range(heads):
            h = c * heads + a
            o_ref[:, h * HD : (h + 1) * HD] = out[a * TOK : (a + 1) * TOK]


def self_attend(q, near, far, core_near, core_far, after):
    in_vmem = pl.BlockSpec(memory_space=pltpu.VMEM)
    return pl.pallas_call(
        self_kernel,
        in_specs=[in_vmem] * 5 + [pl.BlockSpec(memory_space=pl.ANY)],
        out_specs=[in_vmem] * 3,
        out_shape=[
            jax.ShapeDtypeStruct((TOK, WIDTH), BF16),
            jax.ShapeDtypeStruct((1, 2 * HD, TOK), BF16),
            jax.ShapeDtypeStruct((8, HD), F32),
        ],
        compiler_params=params(),
        cost_estimate=cost(6),
        name="self_attend",
    )(q, near, far, core_near, core_far, after)


def along_enc(x, by):
    size = lax.axis_size("enc")
    return lax.ppermute(x, "enc", [(i, (i + by) % size) for i in range(size)])


def along_seq(x, target):
    return lax.ppermute(x, "seq", [(i, target(i)) for i in range(lax.axis_size("seq"))])


def tied(x, *others):
    return lax.optimization_barrier((x, *others))[0]


def on_device(enc_tiles, kv_weight, q_cross, q_self, self_cache, image_range, image_tiles):
    rows = enc_tiles.shape[2]
    sent = -(-rows // HD) * HD
    size = lax.axis_size("seq")
    forward = lambda x: lax.ppermute(x, "seq", [(i, i + 1) for i in range(size - 1)])
    backward = lambda x: lax.ppermute(x, "seq", [(i + 1, i) for i in range(size - 1)])
    cache = self_cache[0]
    got = along_seq(cache, lambda i: i ^ 2)
    q_far = along_enc(q_cross, 2)
    q_up = along_enc(q_cross, 3)
    q_down = along_enc(q_cross, 1)
    q_next = backward(q_cross)
    cache = jnp.concatenate([cache, got], 0)
    tiles, weights = stage(enc_tiles[0, 0], kv_weight, cache)
    got = along_seq(cache, lambda i: i ^ 6)
    cache = jnp.concatenate([cache, tied(got, tiles)], 0)
    got = along_seq(cache, lambda i: i ^ 8)
    q_rest = jnp.stack([q_up, q_down, q_far])
    q_rest_next = backward(q_rest)
    (kv,) = project(
        image_tiles, tiles, weights, (cache, q_rest, q_next), ((0, 1, 3, 2),), sent, 416
    )
    near_cache = jnp.concatenate([cache, tied(got, kv)], 0)
    far_cache = along_seq(near_cache, lambda i: i ^ 24)
    core_near = along_seq(near_cache, lambda i: i ^ 1)
    attend = functools.partial(cross, image_tiles, image_range, kv=kv, rows=rows)
    (own_next,) = attend([(q_next, 0)], picks=(0,), after=(near_cache,), last=size - 1)
    (far_next,) = attend(
        [(q_rest_next, 2)], picks=(3,), after=(own_next, core_near), last=size - 1
    )
    far_prior = forward(far_next)
    (near_next,) = attend(
        [(q_rest_next, 0), (q_rest_next, 1)],
        picks=(1, 2),
        after=(far_next,),
        carry=own_next,
        last=size - 1,
    )
    near_prior = forward(near_next)
    (far,) = attend(
        [(q_rest, 2)], picks=(3,), prior=far_prior, priors=(0,), after=(near_next,)
    )
    far_got = along_enc(far, 2)
    core_far = along_seq(tied(far_cache, far), lambda i: i ^ 1)
    (near,) = attend([(q_cross, 0), (q_rest, 0), (q_rest, 1)], picks=(0, 1, 2), after=(far,))
    mine, up, down = merge(image_range, near, near_prior, (0, 1, 2), far)
    up_got = along_enc(up, 1)
    down_got = along_enc(down, 3)
    self_context, cache_seq, mark = self_attend(
        q_self, near_cache, far_cache, core_near, core_far, up
    )
    return finish([mine, far_got, up_got, down_got], mark), self_context, cache_seq


def solution(mesh):
    return jax.shard_map(
        on_device,
        mesh=mesh,
        in_specs=(
            P("seq", "enc", None, None),
            P(),
            P("seq", "enc"),
            P("seq", "enc"),
            P("enc", "seq", None),
            P("seq", None),
            P(),
        ),
        out_specs=(P("seq", "enc"), P("seq", "enc"), P("enc", None, "seq")),
        check_vma=False,
    )
```

```python
import functools
import math

import jax
import jax.numpy as jnp
from jax import lax
from jax.experimental import pallas as pl
from jax.experimental.pallas import tpu as pltpu
from jax.sharding import PartitionSpec as P

HD = 128
GROUP = 8
TOK = 128
WIDTH = GROUP * HD
STAT = 128
PACK = WIDTH + STAT
NEG = -1e30
EXP2_SCALE = math.log2(math.e) / math.sqrt(HD)
VMEM = 28 * 1024 * 1024
BF16 = jnp.bfloat16
F32 = jnp.float32
COST_UNIT = 1_150_000_000


def cost(microseconds):
    return pl.CostEstimate(
        flops=int(microseconds * COST_UNIT), bytes_accessed=1000, transcendentals=0
    )


def params(limit=VMEM):
    return pltpu.CompilerParams(vmem_limit_bytes=limit)


def stage_kernel(x_hbm, w_hbm, _, x_ref, w_ref, sems):
    copies = [
        pltpu.make_async_copy(x_hbm, x_ref, sems.at[0]),
        pltpu.make_async_copy(w_hbm, w_ref, sems.at[1]),
    ]
    for copy in copies:
        copy.start()
    for copy in copies:
        copy.wait()


def stage(x, w, after):
    anywhere = pl.BlockSpec(memory_space=pl.ANY)
    in_vmem = pl.BlockSpec(memory_space=pltpu.VMEM)
    return pl.pallas_call(
        stage_kernel,
        in_specs=[anywhere] * 3,
        out_specs=[in_vmem] * 2,
        out_shape=[jax.ShapeDtypeStruct(x.shape, BF16), jax.ShapeDtypeStruct(w.shape, BF16)],
        scratch_shapes=[pltpu.SemaphoreType.DMA((2,))],
        compiler_params=params(),
        cost_estimate=cost(4),
        name="stage",
    )(x, w, after)


def project_kernel(tiles_ref, x_ref, w_ref, *refs, offsets, step):
    o_refs = refs[-len(offsets) :]
    enc = lax.axis_index("enc")
    live = enc < tiles_ref[lax.axis_index("seq")]
    rows = x_ref.shape[0]
    sent = o_refs[0].shape[1]

    @pl.when(live)
    def _():
        for o_ref, group in zip(o_refs, offsets):
            for b, offset in enumerate(group):
                g = lax.rem(enc + offset, 4)
                w = w_ref[:, pl.ds(pl.multiple_of(g * 2 * HD, 2 * HD), 2 * HD)]
                for start in range(0, rows, step):
                    end = min(start + step, rows)
                    y = jnp.dot(x_ref[start:end], w, preferred_element_type=F32)
                    if end == rows:
                        y = jnp.concatenate([y, jnp.zeros((sent - rows, 2 * HD), F32)], 0)
                        end = sent
                    o_ref[b, start:end] = y.astype(BF16)


def project(tiles, x, w, after, offsets, sent, step):
    in_vmem = pl.BlockSpec(memory_space=pltpu.VMEM)
    return pl.pallas_call(
        functools.partial(project_kernel, offsets=offsets, step=step),
        in_specs=[pl.BlockSpec(memory_space=pltpu.SMEM), in_vmem, in_vmem]
        + [pl.BlockSpec(memory_space=pl.ANY)] * len(after),
        out_specs=[in_vmem for _ in offsets],
        out_shape=[jax.ShapeDtypeStruct((len(o), sent, 2 * HD), BF16) for o in offsets],
        compiler_params=params(),
        cost_estimate=cost(5.5),
        name="project",
    )(tiles, x, w, *after)


def split_stat(lse):
    hi = lse.astype(BF16)
    rest = lse - hi.astype(F32)
    mid = rest.astype(BF16)
    low = (rest - mid.astype(F32)).astype(BF16)
    return hi, mid, low


def cross_kernel(tiles_ref, range_ref, *refs, waits, count, picks, priors, outputs, rows, last, carried):
    carry_ref = refs[waits - 1] if carried else None
    refs = refs[waits:]
    q_refs = refs[:count]
    kv_ref = refs[count]
    prior_ref = refs[count + 1] if priors else None
    o_refs = refs[-1 - outputs : -1]
    queries = refs[-1]
    padded = kv_ref.shape[1]
    seq = lax.axis_index("seq")
    live = lax.axis_index("enc") < tiles_ref[seq]
    each = (count + carried) // outputs
    if carried:
        o_refs[0][:carried] = carry_ref[...]
    lanes = lax.broadcasted_iota(jnp.int32, (1, HD), 1)

    def sees(image, shape):
        spans = [
            ((range_ref[c, 0] <= image) & (image < range_ref[c, 1])).astype(jnp.int32)
            for c in range(2)
        ]
        token = lax.rem(lax.broadcasted_iota(jnp.int32, shape, 0), TOK)
        return jnp.where(token < TOK // 2, spans[0], spans[1]) != 0

    if not priors:
        live = live & (seq < last)

    @pl.when(jnp.logical_not(live))
    def _():
        for b in range(count):
            o_ref = o_refs[b // each]
            if priors:
                o_ref[b % each, :, :WIDTH] = prior_ref[priors[b], :, :WIDTH]
                o_ref[b % each, :, WIDTH:] = jnp.where(
                    sees(seq - 1, (TOK, STAT)), prior_ref[priors[b], :, WIDTH:].astype(F32), NEG
                ).astype(BF16)
            else:
                o_ref[b + carried, :, :WIDTH] = jnp.zeros((TOK, WIDTH), BF16)
                o_ref[b + carried, :, WIDTH:] = jnp.full((TOK, STAT), NEG, BF16)

    @pl.when(live)
    def _():
        for b in range(count):
            for h in range(GROUP):
                queries[b, h * TOK : (h + 1) * TOK] = q_refs[b][0, :, h * HD : (h + 1) * HD]
        edge = jnp.where(lanes < rows - (padded - HD), 0.0, NEG)
        part = 4
        if priors:
            seen = sees(seq, (part * TOK, 1))
            seen_before = sees(seq - 1, (TOK, GROUP))

        for b in range(count):
            o_ref, at_out = o_refs[(b + carried) // each], (b + carried) % each
            keys = kv_ref[picks[b], :, :HD]
            values = jnp.concatenate([kv_ref[picks[b], :, HD:], jnp.ones((padded, HD), BF16)], 1)
            if priors:
                before = jnp.where(seen_before, stat_of(prior_ref[priors[b]]), NEG)
            tops = jnp.zeros((TOK, STAT), F32)
            sums = jnp.ones((TOK, STAT), F32)
            for c in range(GROUP // part):
                q = queries[b, c * part * TOK : (c + 1) * part * TOK]
                s = lax.dot_general(q, keys, (((1,), (1,)), ((), ())), preferred_element_type=F32)
                s = jnp.concatenate([s[:, : padded - HD], s[:, padded - HD :] + edge], 1)
                m = jnp.max(s, 1, keepdims=True) * EXP2_SCALE
                if priors:
                    prior = jnp.concatenate(
                        [before[:, c * part + a : c * part + a + 1] for a in range(part)], 0
                    )
                    m = jnp.where(seen, jnp.maximum(m, prior), prior)
                p = jnp.exp2(s * EXP2_SCALE - m).astype(BF16)
                mixed = jnp.dot(p, values, preferred_element_type=F32)
                total = mixed[:, HD:]
                mixed = mixed[:, :HD]
                if priors:
                    share = jnp.exp2(prior - m)
                    total = jnp.where(seen, total, 0.0) + share
                    out = jnp.concatenate(
                        [
                            prior_ref[priors[b], :, (c * part + a) * HD : (c * part + a + 1) * HD]
                            for a in range(part)
                        ],
                        0,
                    ).astype(F32)
                    mixed = jnp.where(seen, mixed, 0.0) + out * share
                out = (mixed * (1.0 / total)).astype(BF16)
                for a in range(part):
                    h = c * part + a
                    at = slice(a * TOK, (a + 1) * TOK)
                    o_ref[at_out, :, h * HD : (h + 1) * HD] = out[at]
                    here = lax.rem(lanes, GROUP) == h
                    tops = jnp.where(here, m[at], tops)
                    sums = jnp.where(here, total[at], sums)
            hi, mid, low = split_stat(tops + jnp.log2(sums))
            o_ref[at_out, :, WIDTH:] = jnp.where(
                lanes < GROUP, hi, jnp.where(lanes < 2 * GROUP, mid, low)
            )


def cross(tiles, image_range, queries, kv, picks, rows, prior=None, priors=(), outputs=1, after=(), carry=None, last=None):
    count = len(queries)
    carried = 0 if carry is None else carry.shape[0]
    each = (count + carried) // outputs
    whole = lambda shape: pl.BlockSpec(shape, lambda i, t, r: (0,) * len(shape))
    return pl.pallas_call(
        functools.partial(
            cross_kernel,
            waits=len(after) + min(carried, 1),
            carried=carried,
            count=count,
            picks=picks,
            priors=priors,
            outputs=outputs,
            rows=rows,
            last=lax.axis_size("seq") if last is None else last,
        ),
        grid_spec=pltpu.PrefetchScalarGridSpec(
            num_scalar_prefetch=2,
            grid=(1,),
            in_specs=[pl.BlockSpec(memory_space=pl.ANY)] * len(after)
            + ([whole(carry.shape)] if carried else [])
            + [
                pl.BlockSpec((1, TOK, WIDTH), functools.partial(lambda k, i, t, r: (k, 0, 0), k))
                for _, k in queries
            ]
            + [pl.BlockSpec(memory_space=pltpu.VMEM)]
            + ([whole(prior.shape)] if priors else []),
            out_specs=[whole((each, TOK, PACK))] * outputs,
            scratch_shapes=[pltpu.VMEM((count, GROUP * TOK, HD), BF16)],
        ),
        out_shape=[jax.ShapeDtypeStruct((each, TOK, PACK), BF16)] * outputs,
        compiler_params=params(),
        cost_estimate=cost(2.9 * count),
        name="cross",
    )(
        tiles,
        image_range,
        *after,
        *([carry] if carried else []),
        *[q if q.ndim == 3 else q[None] for q, _ in queries],
        kv,
        *([prior] if priors else []),
    )


def stat_of(packed):
    s = packed[:, WIDTH:].astype(F32)
    return s[:, :GROUP] + s[:, GROUP : 2 * GROUP] + s[:, 2 * GROUP : 3 * GROUP]


def merge_kernel(range_ref, now_ref, prior_ref, *o_refs, picks):
    seq = lax.axis_index("seq")
    first = lax.broadcasted_iota(jnp.int32, (TOK, GROUP), 0) < TOK // 2
    seen = []
    for image in (seq, seq - 1):
        spans = [
            ((range_ref[c, 0] <= image) & (image < range_ref[c, 1])).astype(jnp.int32)
            for c in range(2)
        ]
        seen.append(jnp.where(first, spans[0], spans[1]) != 0)
    lanes = lax.broadcasted_iota(jnp.int32, (1, STAT), 1)
    for b, (pick, o_ref) in enumerate(zip(picks, o_refs)):
        l0 = jnp.where(seen[0], stat_of(now_ref[b]), NEG)
        l1 = jnp.where(seen[1], stat_of(prior_ref[pick]), NEG)
        top = jnp.maximum(l0, l1)
        w0 = jnp.exp2(l0 - top)
        w1 = jnp.exp2(l1 - top)
        total = w0 + w1
        scale = 1.0 / total
        w0 = w0 * scale
        w1 = w1 * scale
        hi, mid, low = split_stat(top + jnp.log2(total))
        o_ref[0, :, WIDTH:] = jnp.concatenate(
            [hi, mid, low, jnp.zeros((TOK, STAT - 3 * GROUP), BF16)], 1
        )
        for h in range(GROUP):
            at = slice(h * HD, (h + 1) * HD)
            o_ref[0, :, at] = (
                now_ref[b, :, at].astype(F32) * w0[:, h : h + 1]
                + prior_ref[pick, :, at].astype(F32) * w1[:, h : h + 1]
            ).astype(BF16)


def merge(image_range, now, prior, picks, after):
    in_vmem = pl.BlockSpec(memory_space=pltpu.VMEM)

    def kernel(range_ref, _, *refs):
        merge_kernel(range_ref, *refs, picks=picks)

    return pl.pallas_call(
        kernel,
        in_specs=[
            pl.BlockSpec(memory_space=pltpu.SMEM),
            pl.BlockSpec(memory_space=pl.ANY),
            in_vmem,
            in_vmem,
        ],
        out_specs=[in_vmem] * len(picks),
        out_shape=[jax.ShapeDtypeStruct((1, TOK, PACK), BF16)] * len(picks),
        compiler_params=params(),
        cost_estimate=cost(2),
        name="merge",
    )(image_range, after, now, prior)


def finish_kernel(*refs):
    parts, o_ref = refs[:4], refs[5]
    stats = [stat_of(part[0]) for part in parts]
    top = functools.reduce(jnp.maximum, stats)
    weights = [jnp.exp2(s - top) for s in stats]
    total = functools.reduce(jnp.add, weights)
    weights = [w / total for w in weights]
    for h in range(GROUP):
        at = slice(h * HD, (h + 1) * HD)
        o_ref[:, at] = functools.reduce(
            jnp.add,
            [part[0, :, at].astype(F32) * w[:, h : h + 1] for part, w in zip(parts, weights)],
        ).astype(BF16)


def finish(parts, after):
    return pl.pallas_call(
        finish_kernel,
        in_specs=[pl.BlockSpec(memory_space=pltpu.VMEM)] * 4 + [pl.BlockSpec(memory_space=pl.ANY)],
        out_specs=pl.BlockSpec(memory_space=pltpu.VMEM),
        out_shape=jax.ShapeDtypeStruct((TOK, WIDTH), BF16),
        compiler_params=params(),
        cost_estimate=cost(1.5),
        name="finish",
    )(*parts, after)


KEY_STEP = 1024


def self_kernel(q_ref, near, far, core_near, core_far, _, o_ref, cache_ref, mark_ref):
    mark_ref[...] = jnp.zeros(mark_ref.shape, F32)
    seq = lax.axis_index("seq")
    z = seq // 8
    y = lax.rem(seq // 2, 4)
    core = lax.rem(seq, 2)
    low = z < 2
    low_z = jnp.where(low, z, 3 - z)

    def order(z_bit):
        at = lax.broadcasted_iota(jnp.int32, (HD, HD), 1)
        feature = lax.broadcasted_iota(jnp.int32, (HD, HD), 0)
        y_step = (at // 8) % 4
        y_step = y_step ^ (y_step // 2)
        held = (
            ((z_bit ^ ((at // 32) % 2)) * 64)
            + ((y ^ y_step) * 16)
            + ((core ^ (at // 64)) * 8)
            + at % 8
        )
        return (held == feature).astype(BF16)

    key_order = order(low_z)
    value_order = order(1 - low_z)

    def keys_at(at):
        return jnp.concatenate(
            [
                lax.select(low, near[:, at], far[:, at]),
                lax.select(low, core_near[:, at], core_far[:, at]),
            ],
            0,
        )

    def values_at(at):
        return jnp.concatenate(
            [
                lax.select(low, far[:, at], near[:, at]),
                lax.select(low, core_far[:, at], core_near[:, at]),
            ],
            0,
        )

    parts = 2
    heads = GROUP // parts
    queries = []
    for c in range(parts):
        q = jnp.concatenate(
            [q_ref[:, (c * heads + a) * HD : (c * heads + a + 1) * HD] for a in range(heads)], 0
        )
        queries.append(jnp.dot(q, key_order, preferred_element_type=F32).astype(BF16))
    mine = pl.ds(pl.multiple_of(seq * TOK, TOK), TOK)
    for slot, permutation, held in ((0, key_order, keys_at), (1, value_order, values_at)):
        cache_ref[0, slot * HD : (slot + 1) * HD, :] = jnp.dot(
            permutation, held(mine), preferred_element_type=F32
        ).astype(BF16)
    rows = heads * TOK

    def step(j, states, masked):
        at = pl.ds(pl.multiple_of(j * KEY_STEP, KEY_STEP), KEY_STEP)
        keys = keys_at(at)
        values = jnp.concatenate([values_at(at), jnp.ones((HD, KEY_STEP), BF16)], 0)
        if masked:
            row = lax.rem(lax.broadcasted_iota(jnp.int32, (rows, KEY_STEP), 0), TOK) + seq * TOK
            allowed = lax.broadcasted_iota(jnp.int32, (rows, KEY_STEP), 1) + j * KEY_STEP <= row
        out = []
        for c in range(parts):
            m, acc = states[c]
            s = jnp.dot(queries[c], keys, preferred_element_type=F32)
            if masked:
                s = jnp.where(allowed, s, NEG)
            new = jnp.maximum(m, jnp.max(s, 1, keepdims=True))
            p = jnp.exp2((s - new) * EXP2_SCALE).astype(BF16)
            acc = acc * jnp.exp2((m - new) * EXP2_SCALE) + lax.dot_general(
                p, values, (((1,), (1,)), ((), ())), preferred_element_type=F32
            )
            out.append((new, acc))
        return tuple(out)

    states = tuple(
        (jnp.full((rows, 1), NEG, F32), jnp.zeros((rows, 2 * HD), F32)) for _ in range(parts)
    )
    full = (seq * TOK) // KEY_STEP
    states = lax.fori_loop(0, full, lambda j, st: step(j, st, False), states)
    states = step(full, states, True)
    for c in range(parts):
        acc = states[c][1]
        out = (acc[:, :HD] * (1.0 / acc[:, HD:])).astype(BF16)
        out = lax.dot_general(
            out, value_order, (((1,), (1,)), ((), ())), preferred_element_type=F32
        ).astype(BF16)
        for a in range(heads):
            h = c * heads + a
            o_ref[:, h * HD : (h + 1) * HD] = out[a * TOK : (a + 1) * TOK]


def self_attend(q, near, far, core_near, core_far, after):
    in_vmem = pl.BlockSpec(memory_space=pltpu.VMEM)
    return pl.pallas_call(
        self_kernel,
        grid=(1,),
        in_specs=[in_vmem] * 5 + [pl.BlockSpec(memory_space=pl.ANY)],
        out_specs=[
            pl.BlockSpec((TOK, WIDTH), lambda i: (0, 0)),
            pl.BlockSpec((1, 2 * HD, TOK), lambda i: (0, 0, 0)),
            pl.BlockSpec((8, HD), lambda i: (0, 0)),
        ],
        out_shape=[
            jax.ShapeDtypeStruct((TOK, WIDTH), BF16),
            jax.ShapeDtypeStruct((1, 2 * HD, TOK), BF16),
            jax.ShapeDtypeStruct((8, HD), F32),
        ],
        compiler_params=params(),
        cost_estimate=cost(6),
        name="self_attend",
    )(q, near, far, core_near, core_far, after)


def along_enc(x, by):
    size = lax.axis_size("enc")
    return lax.ppermute(x, "enc", [(i, (i + by) % size) for i in range(size)])


def along_seq(x, target):
    return lax.ppermute(x, "seq", [(i, target(i)) for i in range(lax.axis_size("seq"))])


def tied(x, *others):
    return lax.optimization_barrier((x, *others))[0]


def on_device(enc_tiles, kv_weight, q_cross, q_self, self_cache, image_range, image_tiles):
    rows = enc_tiles.shape[2]
    sent = -(-rows // HD) * HD
    size = lax.axis_size("seq")
    forward = lambda x: lax.ppermute(x, "seq", [(i, i + 1) for i in range(size - 1)])
    backward = lambda x: lax.ppermute(x, "seq", [(i + 1, i) for i in range(size - 1)])
    cache = self_cache[0]
    got = along_seq(cache, lambda i: i ^ 2)
    q_far = along_enc(q_cross, 2)
    q_up = along_enc(q_cross, 3)
    q_down = along_enc(q_cross, 1)
    q_next = backward(q_cross)
    cache = jnp.concatenate([cache, got], 0)
    tiles, weights = stage(enc_tiles[0, 0], kv_weight, cache)
    got = along_seq(cache, lambda i: i ^ 6)
    cache = jnp.concatenate([cache, tied(got, tiles)], 0)
    got = along_seq(cache, lambda i: i ^ 8)
    q_rest = jnp.stack([q_up, q_down, q_far])
    q_rest_next = backward(q_rest)
    (kv,) = project(
        image_tiles, tiles, weights, (cache, q_rest, q_next), ((0, 1, 3, 2),), sent, 416
    )
    near_cache = jnp.concatenate([cache, tied(got, kv)], 0)
    far_cache = along_seq(near_cache, lambda i: i ^ 24)
    core_near = along_seq(near_cache, lambda i: i ^ 1)
    attend = functools.partial(cross, image_tiles, image_range, kv=kv, rows=rows)
    (own_next,) = attend([(q_next, 0)], picks=(0,), after=(near_cache,), last=size - 1)
    (far_next,) = attend(
        [(q_rest_next, 2)], picks=(3,), after=(own_next, core_near), last=size - 1
    )
    far_prior = forward(far_next)
    (near_next,) = attend(
        [(q_rest_next, 0), (q_rest_next, 1)],
        picks=(1, 2),
        after=(far_next,),
        carry=own_next,
        last=size - 1,
    )
    near_prior = forward(near_next)
    (far,) = attend(
        [(q_rest, 2)], picks=(3,), prior=far_prior, priors=(0,), after=(near_next,)
    )
    far_got = along_enc(far, 2)
    core_far = along_seq(tied(far_cache, far), lambda i: i ^ 1)
    (near,) = attend([(q_cross, 0), (q_rest, 0), (q_rest, 1)], picks=(0, 1, 2), after=(far,))
    mine, up, down = merge(image_range, near, near_prior, (0, 1, 2), far)
    up_got = along_enc(up, 1)
    down_got = along_enc(down, 3)
    self_context, cache_seq, mark = self_attend(
        q_self, near_cache, far_cache, core_near, core_far, up
    )
    return finish([mine, far_got, up_got, down_got], mark), self_context, cache_seq


def solution(mesh):
    return jax.shard_map(
        on_device,
        mesh=mesh,
        in_specs=(
            P("seq", "enc", None, None),
            P(),
            P("seq", "enc"),
            P("seq", "enc"),
            P("enc", "seq", None),
            P("seq", None),
            P(),
        ),
        out_specs=(P("seq", "enc"), P("seq", "enc"), P("enc", None, "seq")),
        check_vma=False,
    )
```

```python
import functools
import math

import jax
import jax.numpy as jnp
from jax import lax
from jax.experimental import pallas as pl
from jax.experimental.pallas import tpu as pltpu
from jax.sharding import PartitionSpec as P

HD = 128
GROUP = 8
TOK = 128
WIDTH = GROUP * HD
STAT = 128
PACK = WIDTH + STAT
NEG = -1e30
EXP2_SCALE = math.log2(math.e) / math.sqrt(HD)
VMEM = 28 * 1024 * 1024
BF16 = jnp.bfloat16
F32 = jnp.float32
COST_UNIT = 1_150_000_000


def cost(microseconds):
    return pl.CostEstimate(
        flops=int(microseconds * COST_UNIT), bytes_accessed=1000, transcendentals=0
    )


def params(limit=VMEM):
    return pltpu.CompilerParams(vmem_limit_bytes=limit)


def stage_kernel(x_hbm, w_hbm, _, x_ref, w_ref, sems):
    copies = [
        pltpu.make_async_copy(x_hbm, x_ref, sems.at[0]),
        pltpu.make_async_copy(w_hbm, w_ref, sems.at[1]),
    ]
    for copy in copies:
        copy.start()
    for copy in copies:
        copy.wait()


def stage(x, w, after):
    anywhere = pl.BlockSpec(memory_space=pl.ANY)
    in_vmem = pl.BlockSpec(memory_space=pltpu.VMEM)
    return pl.pallas_call(
        stage_kernel,
        in_specs=[anywhere] * 3,
        out_specs=[in_vmem] * 2,
        out_shape=[jax.ShapeDtypeStruct(x.shape, BF16), jax.ShapeDtypeStruct(w.shape, BF16)],
        scratch_shapes=[pltpu.SemaphoreType.DMA((2,))],
        compiler_params=params(),
        cost_estimate=cost(4),
        name="stage",
    )(x, w, after)


def project_kernel(tiles_ref, x_ref, w_ref, *refs, offsets, step):
    o_refs = refs[-len(offsets) :]
    enc = lax.axis_index("enc")
    live = enc < tiles_ref[lax.axis_index("seq")]
    rows = x_ref.shape[0]
    sent = o_refs[0].shape[1]

    @pl.when(live)
    def _():
        for o_ref, group in zip(o_refs, offsets):
            for b, offset in enumerate(group):
                g = lax.rem(enc + offset, 4)
                w = w_ref[:, pl.ds(pl.multiple_of(g * 2 * HD, 2 * HD), 2 * HD)]
                for start in range(0, rows, step):
                    end = min(start + step, rows)
                    y = jnp.dot(x_ref[start:end], w, preferred_element_type=F32)
                    if end == rows:
                        y = jnp.concatenate([y, jnp.zeros((sent - rows, 2 * HD), F32)], 0)
                        end = sent
                    o_ref[b, start:end] = y.astype(BF16)


def project(tiles, x, w, after, offsets, sent, step):
    in_vmem = pl.BlockSpec(memory_space=pltpu.VMEM)
    return pl.pallas_call(
        functools.partial(project_kernel, offsets=offsets, step=step),
        in_specs=[pl.BlockSpec(memory_space=pltpu.SMEM), in_vmem, in_vmem]
        + [pl.BlockSpec(memory_space=pl.ANY)] * len(after),
        out_specs=[in_vmem for _ in offsets],
        out_shape=[jax.ShapeDtypeStruct((len(o), sent, 2 * HD), BF16) for o in offsets],
        compiler_params=params(),
        cost_estimate=cost(5.5),
        name="project",
    )(tiles, x, w, *after)


def split_stat(lse):
    hi = lse.astype(BF16)
    rest = lse - hi.astype(F32)
    mid = rest.astype(BF16)
    low = (rest - mid.astype(F32)).astype(BF16)
    return hi, mid, low


def cross_kernel(tiles_ref, range_ref, *refs, waits, count, picks, priors, outputs, rows, last, carried):
    carry_ref = refs[waits - 1] if carried else None
    refs = refs[waits:]
    q_refs = refs[:count]
    kv_ref = refs[count]
    prior_ref = refs[count + 1] if priors else None
    o_refs = refs[-1 - outputs : -1]
    queries = refs[-1]
    padded = kv_ref.shape[1]
    seq = lax.axis_index("seq")
    live = lax.axis_index("enc") < tiles_ref[seq]
    each = (count + carried) // outputs
    if carried:
        o_refs[0][:carried] = carry_ref[...]
    lanes = lax.broadcasted_iota(jnp.int32, (1, HD), 1)

    def sees(image, shape):
        spans = [
            ((range_ref[c, 0] <= image) & (image < range_ref[c, 1])).astype(jnp.int32)
            for c in range(2)
        ]
        token = lax.rem(lax.broadcasted_iota(jnp.int32, shape, 0), TOK)
        return jnp.where(token < TOK // 2, spans[0], spans[1]) != 0

    if not priors:
        live = live & (seq < last)

    @pl.when(jnp.logical_not(live))
    def _():
        for b in range(count):
            o_ref = o_refs[b // each]
            if priors:
                o_ref[b % each, :, :WIDTH] = prior_ref[priors[b], :, :WIDTH]
                o_ref[b % each, :, WIDTH:] = jnp.where(
                    sees(seq - 1, (TOK, STAT)), prior_ref[priors[b], :, WIDTH:].astype(F32), NEG
                ).astype(BF16)
            else:
                o_ref[b + carried, :, :WIDTH] = jnp.zeros((TOK, WIDTH), BF16)
                o_ref[b + carried, :, WIDTH:] = jnp.full((TOK, STAT), NEG, BF16)

    @pl.when(live)
    def _():
        for b in range(count):
            for h in range(GROUP):
                queries[b, h * TOK : (h + 1) * TOK] = q_refs[b][0, :, h * HD : (h + 1) * HD]
        edge = jnp.where(lanes < rows - (padded - HD), 0.0, NEG)
        part = 4
        if priors:
            seen = sees(seq, (part * TOK, 1))
            seen_before = sees(seq - 1, (TOK, GROUP))

        for b in range(count):
            o_ref, at_out = o_refs[(b + carried) // each], (b + carried) % each
            keys = kv_ref[picks[b], :, :HD]
            values = jnp.concatenate([kv_ref[picks[b], :, HD:], jnp.ones((padded, HD), BF16)], 1)
            if priors:
                before = jnp.where(seen_before, stat_of(prior_ref[priors[b]]), NEG)
            tops = jnp.zeros((TOK, STAT), F32)
            sums = jnp.ones((TOK, STAT), F32)
            for c in range(GROUP // part):
                q = queries[b, c * part * TOK : (c + 1) * part * TOK]
                s = lax.dot_general(q, keys, (((1,), (1,)), ((), ())), preferred_element_type=F32)
                s = jnp.concatenate([s[:, : padded - HD], s[:, padded - HD :] + edge], 1)
                m = jnp.max(s, 1, keepdims=True) * EXP2_SCALE
                if priors:
                    prior = jnp.concatenate(
                        [before[:, c * part + a : c * part + a + 1] for a in range(part)], 0
                    )
                    m = jnp.where(seen, jnp.maximum(m, prior), prior)
                p = jnp.exp2(s * EXP2_SCALE - m).astype(BF16)
                mixed = jnp.dot(p, values, preferred_element_type=F32)
                total = mixed[:, HD:]
                mixed = mixed[:, :HD]
                if priors:
                    share = jnp.exp2(prior - m)
                    total = jnp.where(seen, total, 0.0) + share
                    out = jnp.concatenate(
                        [
                            prior_ref[priors[b], :, (c * part + a) * HD : (c * part + a + 1) * HD]
                            for a in range(part)
                        ],
                        0,
                    ).astype(F32)
                    mixed = jnp.where(seen, mixed, 0.0) + out * share
                out = (mixed * (1.0 / total)).astype(BF16)
                for a in range(part):
                    h = c * part + a
                    at = slice(a * TOK, (a + 1) * TOK)
                    o_ref[at_out, :, h * HD : (h + 1) * HD] = out[at]
                    here = lax.rem(lanes, GROUP) == h
                    tops = jnp.where(here, m[at], tops)
                    sums = jnp.where(here, total[at], sums)
            hi, mid, low = split_stat(tops + jnp.log2(sums))
            o_ref[at_out, :, WIDTH:] = jnp.where(
                lanes < GROUP, hi, jnp.where(lanes < 2 * GROUP, mid, low)
            )


def cross(tiles, image_range, queries, kv, picks, rows, prior=None, priors=(), outputs=1, after=(), carry=None, last=None):
    count = len(queries)
    carried = 0 if carry is None else carry.shape[0]
    each = (count + carried) // outputs
    whole = lambda shape: pl.BlockSpec(shape, lambda i, t, r: (0,) * len(shape))
    return pl.pallas_call(
        functools.partial(
            cross_kernel,
            waits=len(after) + min(carried, 1),
            carried=carried,
            count=count,
            picks=picks,
            priors=priors,
            outputs=outputs,
            rows=rows,
            last=lax.axis_size("seq") if last is None else last,
        ),
        grid_spec=pltpu.PrefetchScalarGridSpec(
            num_scalar_prefetch=2,
            grid=(1,),
            in_specs=[pl.BlockSpec(memory_space=pl.ANY)] * len(after)
            + ([whole(carry.shape)] if carried else [])
            + [
                pl.BlockSpec((1, TOK, WIDTH), functools.partial(lambda k, i, t, r: (k, 0, 0), k))
                for _, k in queries
            ]
            + [pl.BlockSpec(memory_space=pltpu.VMEM)]
            + ([whole(prior.shape)] if priors else []),
            out_specs=[whole((each, TOK, PACK))] * outputs,
            scratch_shapes=[pltpu.VMEM((count, GROUP * TOK, HD), BF16)],
        ),
        out_shape=[jax.ShapeDtypeStruct((each, TOK, PACK), BF16)] * outputs,
        compiler_params=params(),
        cost_estimate=cost(2.9 * count),
        name="cross",
    )(
        tiles,
        image_range,
        *after,
        *([carry] if carried else []),
        *[q if q.ndim == 3 else q[None] for q, _ in queries],
        kv,
        *([prior] if priors else []),
    )


def stat_of(packed):
    s = packed[:, WIDTH:].astype(F32)
    return s[:, :GROUP] + s[:, GROUP : 2 * GROUP] + s[:, 2 * GROUP : 3 * GROUP]


def merge_kernel(range_ref, now_ref, prior_ref, *o_refs, picks):
    seq = lax.axis_index("seq")
    first = lax.broadcasted_iota(jnp.int32, (TOK, GROUP), 0) < TOK // 2
    seen = []
    for image in (seq, seq - 1):
        spans = [
            ((range_ref[c, 0] <= image) & (image < range_ref[c, 1])).astype(jnp.int32)
            for c in range(2)
        ]
        seen.append(jnp.where(first, spans[0], spans[1]) != 0)
    lanes = lax.broadcasted_iota(jnp.int32, (1, STAT), 1)
    for b, (pick, o_ref) in enumerate(zip(picks, o_refs)):
        l0 = jnp.where(seen[0], stat_of(now_ref[b]), NEG)
        l1 = jnp.where(seen[1], stat_of(prior_ref[pick]), NEG)
        top = jnp.maximum(l0, l1)
        w0 = jnp.exp2(l0 - top)
        w1 = jnp.exp2(l1 - top)
        total = w0 + w1
        scale = 1.0 / total
        w0 = w0 * scale
        w1 = w1 * scale
        hi, mid, low = split_stat(top + jnp.log2(total))
        o_ref[0, :, WIDTH:] = jnp.concatenate(
            [hi, mid, low, jnp.zeros((TOK, STAT - 3 * GROUP), BF16)], 1
        )
        for h in range(GROUP):
            at = slice(h * HD, (h + 1) * HD)
            o_ref[0, :, at] = (
                now_ref[b, :, at].astype(F32) * w0[:, h : h + 1]
                + prior_ref[pick, :, at].astype(F32) * w1[:, h : h + 1]
            ).astype(BF16)


def merge(image_range, now, prior, picks, after):
    in_vmem = pl.BlockSpec(memory_space=pltpu.VMEM)

    def kernel(range_ref, _, *refs):
        merge_kernel(range_ref, *refs, picks=picks)

    return pl.pallas_call(
        kernel,
        in_specs=[
            pl.BlockSpec(memory_space=pltpu.SMEM),
            pl.BlockSpec(memory_space=pl.ANY),
            in_vmem,
            in_vmem,
        ],
        out_specs=[in_vmem] * len(picks),
        out_shape=[jax.ShapeDtypeStruct((1, TOK, PACK), BF16)] * len(picks),
        compiler_params=params(),
        cost_estimate=cost(2),
        name="merge",
    )(image_range, after, now, prior)


def finish_kernel(*refs):
    parts, o_ref = refs[:4], refs[5]
    stats = [stat_of(part[0]) for part in parts]
    top = functools.reduce(jnp.maximum, stats)
    weights = [jnp.exp2(s - top) for s in stats]
    total = functools.reduce(jnp.add, weights)
    weights = [w / total for w in weights]
    for h in range(GROUP):
        at = slice(h * HD, (h + 1) * HD)
        o_ref[:, at] = functools.reduce(
            jnp.add,
            [part[0, :, at].astype(F32) * w[:, h : h + 1] for part, w in zip(parts, weights)],
        ).astype(BF16)


def finish(parts, after):
    return pl.pallas_call(
        finish_kernel,
        in_specs=[pl.BlockSpec(memory_space=pltpu.VMEM)] * 4 + [pl.BlockSpec(memory_space=pl.ANY)],
        out_specs=pl.BlockSpec(memory_space=pltpu.VMEM),
        out_shape=jax.ShapeDtypeStruct((TOK, WIDTH), BF16),
        compiler_params=params(),
        cost_estimate=cost(1.5),
        name="finish",
    )(*parts, after)


KEY_STEP = 2048


def self_kernel(q_ref, near, far, core_near, core_far, _, o_ref, cache_ref, mark_ref):
    mark_ref[...] = jnp.zeros(mark_ref.shape, F32)
    seq = lax.axis_index("seq")
    z = seq // 8
    y = lax.rem(seq // 2, 4)
    core = lax.rem(seq, 2)
    low = z < 2
    low_z = jnp.where(low, z, 3 - z)

    def order(z_bit):
        at = lax.broadcasted_iota(jnp.int32, (HD, HD), 1)
        feature = lax.broadcasted_iota(jnp.int32, (HD, HD), 0)
        y_step = (at // 8) % 4
        y_step = y_step ^ (y_step // 2)
        held = (
            ((z_bit ^ ((at // 32) % 2)) * 64)
            + ((y ^ y_step) * 16)
            + ((core ^ (at // 64)) * 8)
            + at % 8
        )
        return (held == feature).astype(BF16)

    key_order = order(low_z)
    value_order = order(1 - low_z)

    def keys_at(at):
        return jnp.concatenate(
            [
                lax.select(low, near[:, at], far[:, at]),
                lax.select(low, core_near[:, at], core_far[:, at]),
            ],
            0,
        )

    def values_at(at):
        return jnp.concatenate(
            [
                lax.select(low, far[:, at], near[:, at]),
                lax.select(low, core_far[:, at], core_near[:, at]),
            ],
            0,
        )

    parts = 2
    heads = GROUP // parts
    queries = []
    for c in range(parts):
        q = jnp.concatenate(
            [q_ref[:, (c * heads + a) * HD : (c * heads + a + 1) * HD] for a in range(heads)], 0
        )
        queries.append(jnp.dot(q, key_order, preferred_element_type=F32).astype(BF16))
    mine = pl.ds(pl.multiple_of(seq * TOK, TOK), TOK)
    for slot, permutation, held in ((0, key_order, keys_at), (1, value_order, values_at)):
        cache_ref[0, slot * HD : (slot + 1) * HD, :] = jnp.dot(
            permutation, held(mine), preferred_element_type=F32
        ).astype(BF16)
    rows = heads * TOK

    def step(j, states, masked):
        at = pl.ds(pl.multiple_of(j * KEY_STEP, KEY_STEP), KEY_STEP)
        keys = keys_at(at)
        values = jnp.concatenate([values_at(at), jnp.ones((HD, KEY_STEP), BF16)], 0)
        if masked:
            row = lax.rem(lax.broadcasted_iota(jnp.int32, (rows, KEY_STEP), 0), TOK) + seq * TOK
            allowed = lax.broadcasted_iota(jnp.int32, (rows, KEY_STEP), 1) + j * KEY_STEP <= row
        out = []
        for c in range(parts):
            m, acc = states[c]
            s = jnp.dot(queries[c], keys, preferred_element_type=F32)
            if masked:
                s = jnp.where(allowed, s, NEG)
            new = jnp.maximum(m, jnp.max(s, 1, keepdims=True))
            p = jnp.exp2((s - new) * EXP2_SCALE).astype(BF16)
            acc = acc * jnp.exp2((m - new) * EXP2_SCALE) + lax.dot_general(
                p, values, (((1,), (1,)), ((), ())), preferred_element_type=F32
            )
            out.append((new, acc))
        return tuple(out)

    states = tuple(
        (jnp.full((rows, 1), NEG, F32), jnp.zeros((rows, 2 * HD), F32)) for _ in range(parts)
    )
    full = (seq * TOK) // KEY_STEP
    states = lax.fori_loop(0, full, lambda j, st: step(j, st, False), states)
    states = step(full, states, True)
    for c in range(parts):
        acc = states[c][1]
        out = (acc[:, :HD] * (1.0 / acc[:, HD:])).astype(BF16)
        out = lax.dot_general(
            out, value_order, (((1,), (1,)), ((), ())), preferred_element_type=F32
        ).astype(BF16)
        for a in range(heads):
            h = c * heads + a
            o_ref[:, h * HD : (h + 1) * HD] = out[a * TOK : (a + 1) * TOK]


def self_attend(q, near, far, core_near, core_far, after):
    in_vmem = pl.BlockSpec(memory_space=pltpu.VMEM)
    return pl.pallas_call(
        self_kernel,
        grid=(1,),
        in_specs=[in_vmem] * 5 + [pl.BlockSpec(memory_space=pl.ANY)],
        out_specs=[
            pl.BlockSpec((TOK, WIDTH), lambda i: (0, 0)),
            pl.BlockSpec((1, 2 * HD, TOK), lambda i: (0, 0, 0)),
            pl.BlockSpec((8, HD), lambda i: (0, 0)),
        ],
        out_shape=[
            jax.ShapeDtypeStruct((TOK, WIDTH), BF16),
            jax.ShapeDtypeStruct((1, 2 * HD, TOK), BF16),
            jax.ShapeDtypeStruct((8, HD), F32),
        ],
        compiler_params=params(),
        cost_estimate=cost(6),
        name="self_attend",
    )(q, near, far, core_near, core_far, after)


def along_enc(x, by):
    size = lax.axis_size("enc")
    return lax.ppermute(x, "enc", [(i, (i + by) % size) for i in range(size)])


def along_seq(x, target):
    return lax.ppermute(x, "seq", [(i, target(i)) for i in range(lax.axis_size("seq"))])


def tied(x, *others):
    return lax.optimization_barrier((x, *others))[0]


def on_device(enc_tiles, kv_weight, q_cross, q_self, self_cache, image_range, image_tiles):
    rows = enc_tiles.shape[2]
    sent = -(-rows // HD) * HD
    size = lax.axis_size("seq")
    forward = lambda x: lax.ppermute(x, "seq", [(i, i + 1) for i in range(size - 1)])
    backward = lambda x: lax.ppermute(x, "seq", [(i + 1, i) for i in range(size - 1)])
    cache = self_cache[0]
    got = along_seq(cache, lambda i: i ^ 2)
    q_far = along_enc(q_cross, 2)
    q_up = along_enc(q_cross, 3)
    q_down = along_enc(q_cross, 1)
    q_next = backward(q_cross)
    cache = jnp.concatenate([cache, got], 0)
    tiles, weights = stage(enc_tiles[0, 0], kv_weight, cache)
    got = along_seq(cache, lambda i: i ^ 6)
    cache = jnp.concatenate([cache, tied(got, tiles)], 0)
    got = along_seq(cache, lambda i: i ^ 8)
    q_rest = jnp.stack([q_up, q_down, q_far])
    q_rest_next = backward(q_rest)
    (kv,) = project(
        image_tiles, tiles, weights, (cache, q_rest, q_next), ((0, 1, 3, 2),), sent, 416
    )
    near_cache = jnp.concatenate([cache, tied(got, kv)], 0)
    far_cache = along_seq(near_cache, lambda i: i ^ 24)
    core_near = along_seq(near_cache, lambda i: i ^ 1)
    attend = functools.partial(cross, image_tiles, image_range, kv=kv, rows=rows)
    (own_next,) = attend([(q_next, 0)], picks=(0,), after=(near_cache,), last=size - 1)
    (far_next,) = attend(
        [(q_rest_next, 2)], picks=(3,), after=(own_next, core_near), last=size - 1
    )
    far_prior = forward(far_next)
    (near_next,) = attend(
        [(q_rest_next, 0), (q_rest_next, 1)],
        picks=(1, 2),
        after=(far_next,),
        carry=own_next,
        last=size - 1,
    )
    near_prior = forward(near_next)
    (far,) = attend(
        [(q_rest, 2)], picks=(3,), prior=far_prior, priors=(0,), after=(near_next,)
    )
    far_got = along_enc(far, 2)
    core_far = along_seq(tied(far_cache, far), lambda i: i ^ 1)
    (near,) = attend([(q_cross, 0), (q_rest, 0), (q_rest, 1)], picks=(0, 1, 2), after=(far,))
    mine, up, down = merge(image_range, near, near_prior, (0, 1, 2), far)
    up_got = along_enc(up, 1)
    down_got = along_enc(down, 3)
    self_context, cache_seq, mark = self_attend(
        q_self, near_cache, far_cache, core_near, core_far, up
    )
    return finish([mine, far_got, up_got, down_got], mark), self_context, cache_seq


def solution(mesh):
    return jax.shard_map(
        on_device,
        mesh=mesh,
        in_specs=(
            P("seq", "enc", None, None),
            P(),
            P("seq", "enc"),
            P("seq", "enc"),
            P("enc", "seq", None),
            P("seq", None),
            P(),
        ),
        out_specs=(P("seq", "enc"), P("seq", "enc"), P("enc", None, "seq")),
        check_vma=False,
    )
```
